32 devices in a mesh: dp: 8 (over y, x, core), fsdp: 4 (over z).
Axes of the slice: x: 2, y: 2, z: 4, core: 2. Of those that a mesh axis runs over, the one named last changes fastest.
Arguments:
- hidden: bfloat16 [16, 1024, 768], P('dp', 'fsdp'), may hold values from -6 to 6
- skip_tokens: bfloat16 [16, 1024, 768], P('dp', 'fsdp'), may hold values from -6 to 6
- backbone_cotangent: bfloat16 [16, 1024, 768], P('dp', 'fsdp'), may hold values from -6 to 6
- head_cotangent: bfloat16 [16, 1024, 768], P('dp', 'fsdp'), may hold values from -6 to 6
- starts: int32 [16, 8], P('dp'), may hold values from 0 to 1023, as said below
- positives: int32 [128], replicated, may hold values from 0 to 127, as said below
- qkv_weight: bfloat16 [2, 768, 2304], P(None, ('dp', 'fsdp')), may hold values from -0.3125 to 0.3125
- qv_bias: bfloat16 [2, 1536], P(None, ('dp', 'fsdp')), may hold values from -3 to 3
- attn_weight: bfloat16 [2, 768, 768], P(None, ('dp', 'fsdp')), may hold values from -1.25 to 1.25
- attn_bias: bfloat16 [2, 768], P(None, ('dp', 'fsdp')), may hold values from -2 to 2
- attn_gain: bfloat16 [2, 768], P(None, ('dp', 'fsdp')), may hold values from 0.5 to 1.5
- attn_shift: bfloat16 [2, 768], P(None, ('dp', 'fsdp')), may hold values from -2 to 2
- inner_weight: bfloat16 [2, 768, 3072], P(None, ('dp', 'fsdp')), may hold values from -0.21875 to 0.21875
- inner_bias: bfloat16 [2, 3072], P(None, ('dp', 'fsdp')), may hold values from -3 to 3
- outer_weight: bfloat16 [2, 3072, 768], P(None, ('dp', 'fsdp')), may hold values from -0.21875 to 0.21875
- outer_bias: bfloat16 [2, 768], P(None, ('dp', 'fsdp')), may hold values from -2 to 2
- ffn_gain: bfloat16 [2, 768], P(None, ('dp', 'fsdp')), may hold values from 0.5 to 1.5
- ffn_shift: bfloat16 [2, 768], P(None, ('dp', 'fsdp')), may hold values from -2 to 2
Outputs:
- contrast_loss: float32 [], replicated
- backbone_out: bfloat16 [16, 1024, 768], P('dp', 'fsdp')
- head_out: bfloat16 [16, 1024, 768], P('dp', 'fsdp')
- grad_hidden: float32 [16, 1024, 768], P('dp', 'fsdp')
- grad_skip_tokens: float32 [16, 1024, 768], P('dp', 'fsdp')
- grad_qkv_weight: float32 [2, 768, 2304], P(None, ('dp', 'fsdp'))
- grad_qv_bias: float32 [2, 1536], P(None, ('dp', 'fsdp'))
- grad_attn_weight: float32 [2, 768, 768], P(None, ('dp', 'fsdp'))
- grad_attn_bias: float32 [2, 768], P(None, ('dp', 'fsdp'))
- grad_attn_gain: float32 [2, 768], P(None, ('dp', 'fsdp'))
- grad_attn_shift: float32 [2, 768], P(None, ('dp', 'fsdp'))
- grad_inner_weight: float32 [2, 768, 3072], P(None, ('dp', 'fsdp'))
- grad_inner_bias: float32 [2, 3072], P(None, ('dp', 'fsdp'))
- grad_outer_weight: float32 [2, 3072, 768], P(None, ('dp', 'fsdp'))
- grad_outer_bias: float32 [2, 768], P(None, ('dp', 'fsdp'))
- grad_ffn_gain: float32 [2, 768], P(None, ('dp', 'fsdp'))
- grad_ffn_shift: float32 [2, 768], P(None, ('dp', 'fsdp'))
The draws below stay inside these ranges and needn't reach their ends.
Inputs may be any that keep to these rules, and one draw needn't show every extreme that they name: In each row the 8 starts rise strictly from 0. A passage covers the positions from its start up to the next start or the row's end; its first token is its CLS token. Passage p is segment p % 8 of row p // 8. positives is a permutation of the passages with positives[p] != p.
All inputs are finite; a program needn't handle non-finite values.
Results may differ from the reference program's by a relative error of at most 0.015.
The reference program's roundings to bfloat16 on the way count: a program that leaves them out, or rounds other values in their place, can miss the bound.
Values may be sent and summed in bfloat16 or wider, within the bound.
No kernel may reach another device: no remote copies, remote signals or barrier semaphores. Data moves between devices by JAX's collectives and lax.ppermute only.
A program may use at most 384 MiB of HBM per device.

```python
import jax
import jax.numpy as jnp
from jax import lax

D = 768
HEADS = 12
HEAD_DIM = 64
FF = 3072
SEQ = 1024
SEGS = 8
ROWS = 16
PASSAGES = 128


def draw_starts(key, part):
    row_keys = jax.random.split(key, ROWS)

    def one_row(row_key):
        chosen = jax.random.permutation(row_key, SEQ - 1)[:SEGS - 1].astype(jnp.int32) + 1
        return jnp.concatenate([jnp.zeros((1,), jnp.int32), jnp.sort(chosen).astype(jnp.int32)])
    return jax.vmap(one_row)(row_keys)


def draw_positives(key, part):
    ordering = jax.random.permutation(key, PASSAGES).astype(jnp.int32)
    return jnp.zeros((PASSAGES,), jnp.int32).at[ordering].set(jnp.roll(ordering, -1))


def shard_levels(rng, extent, pieces, smallest, largest):
    factor_of = 1.0
    for position, blocks in pieces:
        heights = jax.random.uniform(jax.random.fold_in(jax.random.fold_in(rng, 6), position), (blocks,), jnp.float32, smallest / len(pieces), largest / len(pieces))
        factor_of = factor_of * jnp.repeat(jnp.exp(heights), extent[position] // blocks).reshape((-1,) + (1,) * (len(extent) - 1 - position))
    return factor_of


def normal_values(rng, dims, deviation, bound, cuts=(), kind=jnp.bfloat16):
    entries = jax.random.normal(rng, dims, jnp.float32) * deviation
    if len(cuts) > 0:
        entries = shard_levels(rng, dims, cuts, -0.22, 0.18) * entries
    return jnp.clip(entries, min=-bound, max=bound).astype(kind)


def setup_inputs(seed: int = 0) -> dict:
    key_list = jax.random.split(jax.random.key(seed), 19)
    return {
        "hidden": normal_values(key_list[0], (ROWS, SEQ, D), 1.0, 6.0, ((0, 8), (1, 4))),
        "skip_tokens": normal_values(key_list[1], (ROWS, SEQ, D), 1.0, 6.0, ((0, 8), (1, 4))),
        "backbone_cotangent": normal_values(key_list[2], (ROWS, SEQ, D), 1.0, 6.0, ((0, 8), (1, 4))),
        "head_cotangent": normal_values(key_list[3], (ROWS, SEQ, D), 1.0, 6.0, ((0, 8), (1, 4))),
        "starts": draw_starts(jax.random.fold_in(key_list[18], 71), 0),
        "positives": draw_positives(jax.random.fold_in(key_list[18], 71), 0),
        "qkv_weight": normal_values(key_list[6], (2, D, 3 * D), (D // 2) ** -0.5, 0.3125, ((1, 32),)),
        "qv_bias": normal_values(key_list[7], (2, 2 * D), 0.5, 3.0, ((1, 32),)),
        "attn_weight": normal_values(key_list[8], (2, D, D), (D // 32) ** -0.5, 1.25, ((1, 32),)),
        "attn_bias": normal_values(key_list[9], (2, D), 0.3, 2.0, ((1, 32),)),
        "attn_gain": jnp.clip(1.0 + 0.1 * jax.random.normal(key_list[10], (2, D), jnp.float32), 0.5, 1.5).astype(jnp.bfloat16),
        "attn_shift": normal_values(key_list[11], (2, D), 0.3, 2.0, ((1, 32),)),
        "inner_weight": normal_values(key_list[12], (2, D, FF), D ** -0.5, 0.21875, ((1, 32),)),
        "inner_bias": normal_values(key_list[13], (2, FF), 0.5, 3.0, ((1, 32),)),
        "outer_weight": normal_values(key_list[14], (2, FF, D), (FF // 4) ** -0.5, 0.21875, ((1, 32),)),
        "outer_bias": normal_values(key_list[15], (2, D), 0.3, 2.0, ((1, 32),)),
        "ffn_gain": jnp.clip(1.0 + 0.1 * jax.random.normal(key_list[16], (2, D), jnp.float32), 0.5, 1.5).astype(jnp.bfloat16),
        "ffn_shift": normal_values(key_list[17], (2, D), 0.3, 2.0, ((1, 32),)),
    }


FULL_PRECISION = lax.Precision.HIGHEST
EPS = 1e-12
SOFTMAX_HEAT = 0.02
NEGATIVE = -1e+30

@jax.custom_vjp
def low(v):
    return lax.optimization_barrier(v.astype(jnp.bfloat16)).astype(jnp.float32)

@jax.custom_vjp
def low_back(v):
    return v

def low_keep(v):
    return (low(v), None)

def low_pass(kept, grad):
    return (grad,)

def back_keep(v):
    return (v, None)

def back_low(kept, grad):
    return (low(grad),)
low.defvjp(low_keep, low_pass)
low_back.defvjp(back_keep, back_low)

def layer_norm(residual, norm_gain, norm_shift):
    average = lax.optimization_barrier(jnp.mean(residual, axis=-1, keepdims=True))
    centred = residual - average
    variance = lax.optimization_barrier(jnp.mean(centred * centred, axis=-1, keepdims=True))
    return centred * lax.rsqrt(variance + EPS) * norm_gain + norm_shift

def segment_ids(row_starts, positions):
    return lax.optimization_barrier(jnp.sum((row_starts[:, :, None] <= positions[None, None, :]).astype(jnp.int32), axis=1)) - 1

def layer(inputs, segment, weights):
    qkv_w, qv_b, attn_w, attn_b, attn_g, attn_s, inner_w, inner_b, outer_w, outer_b, ffn_g, ffn_s = weights
    rows, length, feature_width = inputs.shape
    inputs_low = low(inputs)
    qkv = jnp.matmul(inputs_low, qkv_w, precision=FULL_PRECISION)
    queries = low(low_back(qkv[..., :feature_width] + qv_b[:feature_width]))
    keyset = low(low_back(qkv[..., feature_width:2 * feature_width]))
    valueset = low(low_back(qkv[..., 2 * feature_width:] + qv_b[feature_width:]))
    shaped = (rows, length, HEADS, HEAD_DIM)
    scores = jnp.einsum('bqhd,bkhd->bhqk', queries.reshape(shaped), keyset.reshape(shaped), precision=FULL_PRECISION) * HEAD_DIM ** (-0.5)
    scores = low_back(scores)
    allowed = segment[:, None, :, None] == segment[:, None, None, :]
    attn_probs = jax.nn.softmax(jnp.where(allowed, scores, NEGATIVE), axis=-1)
    mixture = jnp.einsum('bhqk,bkhd->bqhd', low(attn_probs), valueset.reshape(shaped), precision=FULL_PRECISION)
    mixture = low(low_back(mixture.reshape(rows, length, feature_width)))
    branch = low_back(jnp.matmul(mixture, attn_w, precision=FULL_PRECISION) + attn_b)
    normed = layer_norm(inputs + branch, attn_g, attn_s)
    inner = low_back(jnp.matmul(low(normed), inner_w, precision=FULL_PRECISION) + inner_b)
    outer = low_back(jnp.matmul(low(jax.nn.gelu(inner, approximate=False)), outer_w, precision=FULL_PRECISION) + outer_b)
    return layer_norm(normed + outer, ffn_g, ffn_s)

def group(inputs, skipped, row_starts, backbone, head):
    length = inputs.shape[1]
    positions = jnp.arange(length, dtype=jnp.int32)
    segment = segment_ids(row_starts, positions)
    is_cls = jnp.any(row_starts[:, :, None] == positions[None, None, :], axis=1)
    first = layer(inputs, segment, backbone)
    second = layer(jnp.where(is_cls[:, :, None], first, skipped), segment, head)
    return (first, second)

def reference(hidden, skip_tokens, backbone_cotangent, head_cotangent, starts, positives, qkv_weight, qv_bias, attn_weight, attn_bias, attn_gain, attn_shift, inner_weight, inner_bias, outer_weight, outer_bias, ffn_gain, ffn_shift):
    params = tuple((param.astype(jnp.float32) for param in (qkv_weight, qv_bias, attn_weight, attn_bias, attn_gain, attn_shift, inner_weight, inner_bias, outer_weight, outer_bias, ffn_gain, ffn_shift)))
    blockwise = jax.checkpoint(group)

    def forward(inputs, skipped, *weights):
        backbone = tuple((weight[0] for weight in weights))
        head = tuple((weight[1] for weight in weights))
        rows = inputs.shape[0]
        length = inputs.shape[1]
        feature_width = inputs.shape[2]
        blocks = rows // 2
        stacked = (inputs.reshape(blocks, 2, length, feature_width), skipped.reshape(blocks, 2, length, feature_width), starts.reshape(blocks, 2, starts.shape[1]))

        def advance(carry, piece):
            return (carry, blockwise(piece[0], piece[1], piece[2], backbone, head))
        _, (first, second) = lax.scan(advance, jnp.float32(0.0), stacked)
        first = first.reshape(rows, length, feature_width)
        second = second.reshape(rows, length, feature_width)
        class_vector = first[jnp.arange(rows, dtype=jnp.int32)[:, None], starts.astype(jnp.int32)].reshape(-1, feature_width)
        count = class_vector.shape[0]
        similarity_scores = jnp.matmul(class_vector, class_vector.T, precision=FULL_PRECISION) / (feature_width * SOFTMAX_HEAT)
        diagonal = jnp.arange(count, dtype=jnp.int32)[:, None] == jnp.arange(count, dtype=jnp.int32)[None, :]
        similarity_scores = jnp.where(diagonal, NEGATIVE, similarity_scores)
        loss_totals = jax.nn.logsumexp(similarity_scores, axis=1)
        picked = similarity_scores[jnp.arange(count, dtype=jnp.int32), positives.astype(jnp.int32)]
        return (jnp.sum(loss_totals - picked), first, second)
    (loss, first, second), pull = jax.vjp(forward, hidden.astype(jnp.float32), skip_tokens.astype(jnp.float32), *params)
    grads = pull((jnp.ones((), jnp.float32), backbone_cotangent.astype(jnp.float32), head_cotangent.astype(jnp.float32)))
    return (loss, first.astype(jnp.bfloat16), second.astype(jnp.bfloat16), grads[0], grads[1], grads[2], grads[3], grads[4], grads[5], grads[6], grads[7], grads[8], grads[9], grads[10], grads[11], grads[12], grads[13])
```

```python
import functools

import jax
import jax.numpy as jnp
from jax import lax
from jax.experimental import pallas as pl
from jax.experimental.pallas import tpu as pltpu
from jax.sharding import PartitionSpec as P

HEADS = 12
HEAD_DIM = 64
SEGS = 8
CORES = 2

EPS = 1e-12
SOFTMAX_HEAT = 0.02
NEGATIVE = -1e30
FULL_PRECISION = lax.Precision.HIGHEST
SCALING = HEAD_DIM ** (-0.5)
PAIR = 2 * HEAD_DIM
BF = jnp.bfloat16
F32 = jnp.float32


def layer_norm(residual, norm_gain, norm_shift):
    average = jnp.mean(residual, axis=-1, keepdims=True)
    centred = residual - average
    inv_std = lax.rsqrt(jnp.mean(centred * centred, axis=-1, keepdims=True) + EPS)
    normed = centred * inv_std
    return (normed * norm_gain + norm_shift, normed, inv_std)


def norm_back(upstream, normed, inv_std, norm_gain):
    scaled = upstream * norm_gain
    return inv_std * (
        scaled
        - jnp.mean(scaled, axis=-1, keepdims=True)
        - normed * jnp.mean(scaled * normed, axis=-1, keepdims=True)
    )


def gelu_both(v):
    phi_cdf = 0.5 * (1.0 + lax.erf(v * 0.7071067811865476))
    phi_pdf = jnp.exp(-0.5 * v * v) * 0.3989422804014327
    return v * phi_cdf, phi_cdf + v * phi_pdf


def matrix_product(first_op, second_op):
    return jnp.dot(first_op, second_op, preferred_element_type=F32)


def left_t(first_op, second_op):
    return lax.dot_general(
        first_op, second_op, (((0,), (0,)), ((), ())), preferred_element_type=F32
    )


def right_t(first_op, second_op):
    return lax.dot_general(
        first_op, second_op, (((1,), (1,)), ((), ())), preferred_element_type=F32
    )


def column_sum(inputs):
    return jnp.sum(inputs.astype(F32), axis=0)


def n_bits(count):
    return count.bit_length() - 1


class Grid:
    def __init__(self, rows_dev):
        self.n_dp = lax.axis_size("dp")
        self.n_f = lax.axis_size("fsdp")
        self.f_bits = n_bits(self.n_f)
        self.d_bits = n_bits(self.n_dp)
        self.dp = lax.axis_index("dp")
        self.f = lax.axis_index("fsdp")
        self.rows_dev = rows_dev
        self.chips_per_row = self.n_f // (CORES * rows_dev)
        self.members = CORES * self.chips_per_row
        self.core = self.dp % CORES
        self.row_in_group = self.f // self.chips_per_row
        self.member = (self.f % self.chips_per_row) * CORES + self.core

    def my_bit(self, bit):
        if bit < self.f_bits:
            return (self.f >> bit) & 1
        return (self.dp >> (bit - self.f_bits)) & 1

    def swap(self, x, bit):
        if bit < self.f_bits:
            return lax.ppermute(x, "fsdp", [(i, i ^ (1 << bit)) for i in range(self.n_f)])
        flip = 1 << (bit - self.f_bits)
        return lax.ppermute(x, "dp", [(i, i ^ flip) for i in range(self.n_dp)])

    def gather_order(self, turned):
        upper = list(range(self.f_bits + 1, self.f_bits + self.d_bits))
        if not turned:
            upper = upper[::-1]
        return list(range(self.f_bits)) + upper + [self.f_bits]

    def gather(self, x, order):
        have, out = [], x
        for bit in order:
            other = self.swap(out, bit)
            mine = self.my_bit(bit) == 0
            place = sum(1 for b in have if b > bit)
            low = jnp.where(mine, out, other)
            high = jnp.where(mine, other, out)
            out = jnp.stack([low, high], axis=place)
            have.append(bit)
        return out.reshape((-1,) + x.shape[1:])

    def scatter(self, x, order, wire=BF):
        left = sorted(order, reverse=True)
        tail = (x.shape[0] >> len(order),) + x.shape[1:]
        out = x.reshape((2,) * len(order) + tail)
        for bit in reversed(order):
            place = left.index(bit)
            low = lax.index_in_dim(out, 0, place, keepdims=False)
            high = lax.index_in_dim(out, 1, place, keepdims=False)
            mine = self.my_bit(bit) == 0
            kept = jnp.where(mine, low, high)
            sent = jnp.where(mine, high, low).astype(wire)
            got = self.swap(sent, bit)
            out = kept.astype(F32) + got.astype(F32)
            left.remove(bit)
            if left:
                out = out.astype(wire)
        return out

    def source(self, k):
        pairs = []
        for d in range(self.n_dp):
            for f in range(self.n_f):
                base, c = d // CORES * CORES, d % CORES
                b = (f + k) % self.rows_dev
                g = f // self.rows_dev
                row = self.rows_dev * c + b
                target_f = row * self.chips_per_row + g // CORES
                target_d = base + g % CORES
                pairs.append((d * self.n_f + f, target_d * self.n_f + target_f))
        return pairs

    def to_rows(self, x):
        got = []
        for k in range(self.rows_dev):
            block = lax.dynamic_index_in_dim(x, (self.f + k) % self.rows_dev, 0, keepdims=False)
            got.append(lax.ppermute(block, ("dp", "fsdp"), self.source(k)))
        got = jnp.stack(got)
        b = self.row_in_group % self.rows_dev
        return jnp.concatenate(
            [
                lax.dynamic_index_in_dim(got, (b - p) % self.rows_dev, 0, keepdims=False)
                for p in range(self.rows_dev)
            ]
        )

    def from_rows(self, y):
        parts = y.reshape((self.rows_dev, -1) + y.shape[1:])
        b = self.row_in_group % self.rows_dev
        got = []
        for k in range(self.rows_dev):
            block = lax.dynamic_index_in_dim(parts, (b - k) % self.rows_dev, 0, keepdims=False)
            back = [(t, s) for s, t in self.source(k)]
            got.append(lax.ppermute(block, ("dp", "fsdp"), back))
        got = jnp.stack(got)
        return jnp.stack(
            [
                lax.dynamic_index_in_dim(got, (row - self.f) % self.rows_dev, 0, keepdims=False)
                for row in range(self.rows_dev)
            ]
        )

    def shift_pairs(self, shift):
        pairs = []
        for d in range(self.n_dp):
            for f in range(self.n_f):
                g = (f % self.chips_per_row) * CORES + d % CORES
                t = (g + shift) % self.members
                td = d // CORES * CORES + t % CORES
                tf = f // self.chips_per_row * self.chips_per_row + t // CORES
                pairs.append((d * self.n_f + f, td * self.n_f + tf))
        return pairs

    def to_member(self, x, shift):
        return lax.ppermute(x, ("dp", "fsdp"), self.shift_pairs(shift))


def dot_nt(a, b):
    return lax.dot_general(a, b, (((1,), (1,)), ((), ())), preferred_element_type=F32)


def dot_nn(a, b):
    return lax.dot_general(a, b, (((1,), (0,)), ((), ())), preferred_element_type=F32)


def dot_tn(a, b):
    return lax.dot_general(a, b, (((0,), (0,)), ((), ())), preferred_element_type=F32)


def head_only(x, head):
    lane = lax.broadcasted_iota(jnp.int32, x.shape, 1)
    keep = (lane >= HEAD_DIM) if head else (lane < HEAD_DIM)
    return jnp.where(keep, x, jnp.zeros_like(x))


def attend_kernel(chunks, q_step, *refs):
    q_ref = refs[0]
    k_refs = refs[1 : 1 + chunks]
    v_refs = refs[1 + chunks : 1 + 2 * chunks]
    seg_q_ref, seg_k_ref, o_ref, lse_ref = refs[1 + 2 * chunks :]
    tokens = q_ref.shape[0]
    for q0 in range(0, tokens, q_step):
        q = q_ref[q0 : q0 + q_step, :]
        seg_q = seg_q_ref[:, q0 : q0 + q_step]
        halves = []
        for head in range(2):
            q_head = head_only(q, head)
            scores = []
            for c in range(chunks):
                s = dot_nt(k_refs[c][...], q_head) * SCALING
                seg_k = seg_k_ref[c * tokens : (c + 1) * tokens, :]
                scores.append(jnp.where(seg_k == seg_q, s, NEGATIVE))
            highest = functools.reduce(
                jnp.maximum, [jnp.max(s, axis=0, keepdims=True) for s in scores]
            )
            powers = [jnp.exp(s - highest) for s in scores]
            total = functools.reduce(
                jnp.add, [jnp.sum(p, axis=0, keepdims=True) for p in powers]
            )
            inverse = 1.0 / total
            mixed = functools.reduce(
                jnp.add,
                [dot_tn(v_refs[c][...], (powers[c] * inverse).astype(BF)) for c in range(chunks)],
            )
            halves.append(mixed[head * HEAD_DIM : (head + 1) * HEAD_DIM, :])
            lse_ref[0, head : head + 1, q0 : q0 + q_step] = highest + jnp.log(total)
        both = jnp.concatenate(halves, axis=0)
        o_ref[q0 : q0 + q_step, :] = both.T.astype(BF)


def attend_back_kernel(chunks, q_step, *refs):
    q_ref = refs[0]
    k_refs = refs[1 : 1 + chunks]
    v_refs = refs[1 + chunks : 1 + 2 * chunks]
    do_ref, lse_ref, seg_q_ref, seg_k_ref = refs[1 + 2 * chunks : 5 + 2 * chunks]
    dq_ref, own_ref = refs[5 + 2 * chunks : 7 + 2 * chunks]
    other_refs = refs[7 + 2 * chunks : 6 + 3 * chunks]
    acc_ref = refs[6 + 3 * chunks]
    tokens = q_ref.shape[0]
    first = True
    for q0 in range(0, tokens, q_step):
        q = q_ref[q0 : q0 + q_step, :]
        do = do_ref[q0 : q0 + q_step, :]
        seg_q = seg_q_ref[:, q0 : q0 + q_step]
        halves = []
        for head in range(2):
            q_head = head_only(q, head)
            do_head = head_only(do, head)
            lse = lse_ref[0, head : head + 1, q0 : q0 + q_step]
            probs, d_probs = [], []
            for c in range(chunks):
                s = dot_nt(k_refs[c][...], q_head) * SCALING
                seg_k = seg_k_ref[c * tokens : (c + 1) * tokens, :]
                s = jnp.where(seg_k == seg_q, s, NEGATIVE)
                probs.append(jnp.exp(s - lse))
                d_probs.append(dot_nt(v_refs[c][...], do_head))
            offset = functools.reduce(
                jnp.add,
                [jnp.sum(p * d, axis=0, keepdims=True) for p, d in zip(probs, d_probs)],
            )
            dq_t = None
            for c in range(chunks):
                ds = (probs[c] * (d_probs[c] - offset)).astype(BF)
                dk = dot_nn(ds, q_head) * SCALING
                dv = dot_nn(probs[c].astype(BF), do_head)
                term = dot_tn(k_refs[c][...], ds)
                dq_t = term if dq_t is None else dq_t + term
                if first:
                    acc_ref[c, 0] = dk
                    acc_ref[c, 1] = dv
                else:
                    acc_ref[c, 0] += dk
                    acc_ref[c, 1] += dv
            first = False
            halves.append(dq_t[head * HEAD_DIM : (head + 1) * HEAD_DIM, :])
        both = jnp.concatenate(halves, axis=0) * SCALING
        dq_ref[q0 : q0 + q_step, :] = both.T.astype(BF)
    own_ref[...] = acc_ref[0]
    for c in range(1, chunks):
        other_refs[c - 1][...] = acc_ref[c].astype(BF)


def attention_specs(qkv, others):
    tokens = qkv.shape[0]
    pairs = HEADS // 2
    block = (tokens, PAIR)
    at = lambda offset: pl.BlockSpec(block, lambda i, offset=offset: (0, offset + i))
    operands = [qkv, qkv] + others + [qkv] + others
    specs = (
        [at(0), at(pairs)]
        + [at(0) for _ in others]
        + [at(2 * pairs)]
        + [at(pairs) for _ in others]
    )
    return operands, specs, tokens, pairs


def attend(qkv, others, seg_q, seg_k):
    operands, specs, tokens, pairs = attention_specs(qkv, others)
    chunks = 1 + len(others)
    length = tokens * chunks
    whole = lambda shape: pl.BlockSpec(shape, lambda i: (0,) * len(shape))
    return pl.pallas_call(
        functools.partial(attend_kernel, chunks, min(256, tokens)),
        grid=(pairs,),
        in_specs=specs + [whole((1, tokens)), whole((length, 1))],
        out_specs=[
            pl.BlockSpec((tokens, PAIR), lambda i: (0, i)),
            pl.BlockSpec((1, 2, tokens), lambda i: (i, 0, 0)),
        ],
        out_shape=[
            jax.ShapeDtypeStruct((tokens, HEADS * HEAD_DIM), BF),
            jax.ShapeDtypeStruct((pairs, 2, tokens), F32),
        ],
        compiler_params=pltpu.CompilerParams(vmem_limit_bytes=40 * 2**20),
        cost_estimate=pl.CostEstimate(
            flops=16 * tokens * length * HEADS * HEAD_DIM,
            bytes_accessed=8 * length * HEADS * HEAD_DIM,
            transcendentals=tokens * length * HEADS,
        ),
        name="attend",
    )(*operands, seg_q, seg_k)


def attend_back(qkv, others, d_mixture, lse, seg_q, seg_k):
    operands, specs, tokens, pairs = attention_specs(qkv, others)
    chunks = 1 + len(others)
    length = tokens * chunks
    width = HEADS * HEAD_DIM
    whole = lambda shape: pl.BlockSpec(shape, lambda i: (0,) * len(shape))
    stacked = pl.BlockSpec((2, tokens, PAIR), lambda i: (0, 0, i))
    out = pl.pallas_call(
        functools.partial(attend_back_kernel, chunks, min(256, tokens)),
        grid=(pairs,),
        in_specs=specs
        + [
            pl.BlockSpec((tokens, PAIR), lambda i: (0, i)),
            pl.BlockSpec((1, 2, tokens), lambda i: (i, 0, 0)),
            whole((1, tokens)),
            whole((length, 1)),
        ],
        out_specs=[pl.BlockSpec((tokens, PAIR), lambda i: (0, i)), stacked]
        + [stacked for _ in others],
        out_shape=[
            jax.ShapeDtypeStruct((tokens, width), BF),
            jax.ShapeDtypeStruct((2, tokens, width), F32),
        ]
        + [jax.ShapeDtypeStruct((2, tokens, width), BF) for _ in others],
        scratch_shapes=[pltpu.VMEM((chunks, 2, tokens, PAIR), F32)],
        compiler_params=pltpu.CompilerParams(vmem_limit_bytes=40 * 2**20),
        cost_estimate=pl.CostEstimate(
            flops=40 * tokens * length * width,
            bytes_accessed=20 * length * width,
            transcendentals=tokens * length * HEADS,
        ),
        name="attend_back",
    )(*operands, d_mixture, lse, seg_q, seg_k)
    return out[0], out[1], out[2:]


def split_small(small, sizes):
    vectors, at = [], 0
    for size in sizes:
        vectors.append(small[:, at : at + size].reshape(-1).astype(F32))
        at += size
    return vectors


def layer_forward(grid, inputs, weights, seg_q, seg_k):
    (qkv_w, attn_w, inner_w, outer_w, qv_b, attn_b, attn_g, attn_s, inner_b, outer_b, ffn_g, ffn_s) = weights
    width = inputs.shape[1]
    x_low = inputs.astype(BF)
    bias = jnp.concatenate([qv_b[:width], jnp.zeros((width,), F32), qv_b[width:]])
    qkv = (matrix_product(x_low, qkv_w) + bias).astype(BF)
    key_value = qkv[:, width:]
    others = [grid.to_member(key_value, shift) for shift in range(1, grid.members)]
    mixture, lse = attend(qkv, others, seg_q, seg_k)
    branch = matrix_product(mixture, attn_w) + attn_b
    normed, normed_one, inv_one = layer_norm(inputs.astype(F32) + branch, attn_g, attn_s)
    normed_low = normed.astype(BF)
    inner = matrix_product(normed_low, inner_w) + inner_b
    active, slope = gelu_both(inner)
    active = active.astype(BF)
    outer = matrix_product(active, outer_w) + outer_b
    output, normed_two, inv_two = layer_norm(normed + outer, ffn_g, ffn_s)
    saved = (x_low, qkv, others, lse, mixture, normed_one, inv_one, normed_low, slope, active, normed_two, inv_two)
    return output, saved


def layer_backward(grid, upstream, weights, saved, seg_q, seg_k):
    (qkv_w, attn_w, inner_w, outer_w, qv_b, attn_b, attn_g, attn_s, inner_b, outer_b, ffn_g, ffn_s) = weights
    (x_low, qkv, others, lse, mixture, normed_one, inv_one, normed_low, slope, active, normed_two, inv_two) = saved
    grad_ffn_g = jnp.sum(upstream * normed_two, axis=0)
    grad_ffn_s = jnp.sum(upstream, axis=0)
    d_second = norm_back(upstream, normed_two, inv_two, ffn_g)
    d_outer = d_second.astype(BF)
    grad_outer_b = column_sum(d_outer)
    grad_outer_w = left_t(active, d_outer).astype(BF)
    d_inner = (right_t(d_outer, outer_w) * slope).astype(BF)
    grad_inner_b = column_sum(d_inner)
    grad_inner_w = left_t(normed_low, d_inner).astype(BF)
    d_normed = right_t(d_inner, inner_w) + d_second
    grad_attn_g = jnp.sum(d_normed * normed_one, axis=0)
    grad_attn_s = jnp.sum(d_normed, axis=0)
    d_first = norm_back(d_normed, normed_one, inv_one, attn_g)
    d_branch = d_first.astype(BF)
    grad_attn_b = column_sum(d_branch)
    grad_attn_w = left_t(mixture, d_branch).astype(BF)
    d_mixture = right_t(d_branch, attn_w).astype(BF)
    d_queries, own, for_others = attend_back(qkv, others, d_mixture, lse, seg_q, seg_k)
    for shift in range(1, grid.members):
        own = own + grid.to_member(for_others[shift - 1], -shift).astype(F32)
    own = own.astype(BF)
    d_qkv = jnp.concatenate([d_queries, own[0], own[1]], axis=1)
    grad_qv_b = jnp.concatenate([column_sum(d_queries), column_sum(own[1])])
    grad_qkv_w = left_t(x_low, d_qkv).astype(BF)
    d_input = right_t(d_qkv, qkv_w) + d_first
    grads = (grad_qkv_w, grad_attn_w, grad_inner_w, grad_outer_w)
    small = (grad_qv_b, grad_attn_b, grad_attn_g, grad_attn_s, grad_inner_b, grad_outer_b, grad_ffn_g, grad_ffn_s)
    return d_input, grads, small


def contrastive(vectors, positives):
    count, width = vectors.shape
    similarity = jnp.dot(vectors, vectors.T, precision=FULL_PRECISION) / (width * SOFTMAX_HEAT)
    ids = jnp.arange(count, dtype=jnp.int32)
    similarity = jnp.where(ids[:, None] == ids[None, :], NEGATIVE, similarity)
    highest = jnp.max(similarity, axis=1, keepdims=True)
    totals = highest + jnp.log(jnp.sum(jnp.exp(similarity - highest), axis=1, keepdims=True))
    positive = positives[:, None] == ids[None, :]
    loss = jnp.sum(totals) - jnp.sum(jnp.where(positive, similarity, 0.0))
    slope = (jnp.exp(similarity - totals) - positive.astype(F32)) / (width * SOFTMAX_HEAT)
    return loss, jnp.dot(slope + slope.T, vectors, precision=FULL_PRECISION)


def body(
    hidden,
    skip_tokens,
    backbone_cotangent,
    head_cotangent,
    starts,
    positives,
    qkv_weight,
    qv_bias,
    attn_weight,
    attn_bias,
    attn_gain,
    attn_shift,
    inner_weight,
    inner_bias,
    outer_weight,
    outer_bias,
    ffn_gain,
    ffn_shift,
):
    rows_dev, local, width = hidden.shape
    grid = Grid(rows_dev)
    tokens = rows_dev * local
    length = tokens * grid.members

    starts_both = jnp.stack([starts, grid.swap(starts, grid.f_bits)])
    from_other = jnp.where(grid.row_in_group // rows_dev == grid.core, 0, 1)
    my_starts = lax.dynamic_index_in_dim(starts_both, from_other, 0, keepdims=False)
    my_starts = lax.dynamic_index_in_dim(
        my_starts, grid.row_in_group % rows_dev, 0, keepdims=False
    )
    place = jnp.arange(tokens, dtype=jnp.int32)
    q_pos = grid.member * tokens + place
    k_pos = jnp.concatenate(
        [
            (grid.member - shift) % grid.members * tokens + place
            for shift in range(grid.members)
        ]
    )
    segment = lambda pos: jnp.sum((my_starts[:, None] <= pos[None, :]).astype(jnp.int32), axis=0) - 1
    seg_q = segment(q_pos)[None, :]
    seg_k = segment(k_pos)[:, None]
    cls_hot = (my_starts[:, None] == q_pos[None, :]).astype(F32)
    is_cls = jnp.any(my_starts[:, None] == q_pos[None, :], axis=0)[:, None]

    order, turned = grid.gather_order(False), grid.gather_order(True)
    x = grid.to_rows(hidden)
    vectors = (qv_bias, attn_bias, attn_gain, attn_shift, inner_bias, outer_bias, ffn_gain, ffn_shift)
    sizes = [v.shape[1] for v in vectors]
    small_own = jnp.concatenate(vectors, axis=1)
    small = grid.gather(small_own[None], order)
    layers = []
    for layer in range(2):
        qkv_w = grid.gather(qkv_weight[layer], order)
        mid = jnp.concatenate([attn_weight[layer], inner_weight[layer]], axis=1)
        mid = grid.gather(mid, turned)
        outer_w = grid.gather(outer_weight[layer], order)
        layers.append(
            (qkv_w, mid[:, :width], mid[:, width:], outer_w, *split_small(small[:, layer], sizes))
        )
    backbone, head = layers
    rest = grid.to_rows(jnp.concatenate([skip_tokens, head_cotangent, backbone_cotangent], axis=2))
    skip, head_cot, backbone_cot = rest[:, :width], rest[:, width : 2 * width], rest[:, 2 * width :]

    first, saved_one = layer_forward(grid, x, backbone, seg_q, seg_k)
    cls_own = jnp.dot(cls_hot, first, precision=FULL_PRECISION)[None]
    head_in = jnp.where(is_cls, first, skip.astype(F32))
    second, saved_two = layer_forward(grid, head_in, head, seg_q, seg_k)

    shared = n_bits(grid.chips_per_row)
    for bit in [grid.f_bits] + list(range(shared)):
        cls_own = cls_own + grid.swap(cls_own, bit)
    cls_order = list(range(shared, grid.f_bits)) + list(range(grid.f_bits + 1, grid.f_bits + grid.d_bits))
    cls_all = grid.gather(cls_own, cls_order).reshape(-1, width)
    contrast_loss, d_cls_all = contrastive(cls_all, positives)
    my_row = grid.dp // CORES * (CORES * rows_dev) + grid.row_in_group
    d_cls = lax.dynamic_slice_in_dim(d_cls_all, my_row * SEGS, SEGS, 0)

    d_head_in, grads_two, small_two = layer_backward(
        grid, head_cot.astype(F32), head, saved_two, seg_q, seg_k
    )
    upstream = (
        backbone_cot.astype(F32)
        + jnp.where(is_cls, d_head_in, 0.0)
        + lax.dot_general(cls_hot, d_cls, (((0,), (0,)), ((), ())), precision=FULL_PRECISION)
    )
    outs = jnp.concatenate(
        [first.astype(BF), second.astype(BF), jnp.where(is_cls, 0.0, d_head_in).astype(BF)], axis=1
    )
    outs = grid.from_rows(outs)
    d_input, grads_one, small_one = layer_backward(grid, upstream, backbone, saved_one, seg_q, seg_k)
    grad_hidden = grid.from_rows(d_input.astype(BF)).astype(F32)

    devices = grid.n_dp * grid.n_f
    scattered = []
    for grad_qkv, grad_attn, grad_inner, grad_outer in (grads_one, grads_two):
        outer_g = grid.scatter(grad_outer, order)
        mid = grid.scatter(jnp.concatenate([grad_attn, grad_inner], axis=1), turned)
        qkv_g = grid.scatter(grad_qkv, order)
        scattered.append((qkv_g, mid[:, :width], mid[:, width:], outer_g))
    small_g = jnp.stack(
        [
            jnp.concatenate([v.reshape(devices, -1) for v in small], axis=1)
            for small in (small_one, small_two)
        ],
        axis=1,
    )
    small_g = grid.scatter(small_g, order, F32)[0]
    cuts, at = [], 0
    for size in sizes:
        cuts.append(small_g[:, at : at + size])
        at += size
    qkv_g, attn_g, inner_g, outer_g = (jnp.stack(pair) for pair in zip(*scattered))
    return (
        contrast_loss,
        outs[:, :, :width],
        outs[:, :, width : 2 * width],
        grad_hidden,
        outs[:, :, 2 * width :].astype(F32),
        qkv_g,
        cuts[0],
        attn_g,
        cuts[1],
        cuts[2],
        cuts[3],
        inner_g,
        cuts[4],
        outer_g,
        cuts[5],
        cuts[6],
        cuts[7],
    )


def solution(mesh):
    rows = P("dp", "fsdp", None)
    matrix = P(None, ("dp", "fsdp"), None)
    vector = P(None, ("dp", "fsdp"))
    params = (
        matrix,
        vector,
        matrix,
        vector,
        vector,
        vector,
        matrix,
        vector,
        matrix,
        vector,
        vector,
        vector,
    )
    return jax.shard_map(
        body,
        mesh=mesh,
        in_specs=(rows, rows, rows, rows, P("dp", None), P()) + params,
        out_specs=(P(), rows, rows, rows, rows) + params,
        check_vma=False,
    )
```

```python
import functools

import jax
import jax.numpy as jnp
from jax import lax
from jax.experimental import pallas as pl
from jax.experimental.pallas import tpu as pltpu
from jax.sharding import PartitionSpec as P

HEADS = 12
HEAD_DIM = 64
SEGS = 8
CORES = 2

EPS = 1e-12
SOFTMAX_HEAT = 0.02
NEGATIVE = -1e30
FULL_PRECISION = lax.Precision.HIGHEST
SCALING = HEAD_DIM ** (-0.5)
PAIR = 2 * HEAD_DIM
BF = jnp.bfloat16
F32 = jnp.float32

GATHER_TICKS, HEAD_TICKS, TAIL_TICKS = 7, 2, 0
PLAN = {
    "g0": ["qkv_one"],
    "g1": ["qkv_one", "ffn_one"],
    "g2": ["qkv_one", "ffn_one"],
    "g3": ["qkv_one", "hidden"],
    "g4": ["qkv_one", "ffn_one"],
    "g5": ["qkv_one", "hidden", "qkv_two"],
    "f0.qkv": ["ffn_one", "qkv_two"],
    "f0.attend": ["ffn_one", "qkv_two", "ffn_two"],
    "f0.normed": ["ffn_one", "qkv_two", "ffn_two"],
    "f0.active": ["skip"],
    "f0.out": [],
    "h0": ["qkv_two", "cls", "ffn_two"],
    "h1": ["qkv_two", "cls", "skip", "cots"],
    "f1.qkv": ["ffn_two", "cls"],
    "f1.attend": ["ffn_two", "cls"],
    "f1.normed": ["ffn_two", "cls"],
    "f1.out": ["cls", "cots"],
    "t": ["outs"],
    "b1.d_outer": ["back_outer_two"],
    "b1.d_inner": ["back_outer_two", "back_inner_two"],
    "b1.d_mixture": ["back_inner_two"],
    "b1.d_queries": ["back_outer_two", "back_inner_two"],
    "b1.d_qkv": ["back_outer_two", "back_inner_two", "back_qkv_two", "outs"],
    "u": ["back_z_two", "back_qkv_two", "skip_back"],
    "b0.d_outer": ["back_outer_one"],
    "b0.d_inner": ["back_z_two", "back_qkv_two", "back_outer_one", "back_inner_one"],
    "b0.d_mixture": ["back_z_two", "back_inner_one"],
    "b0.d_queries": ["back_outer_one", "back_inner_one", "back_qkv_two", "skip_back"],
    "b0.d_qkv": ["back_outer_one", "back_inner_one", "back_qkv_one", "back_qkv_two"],
    "b0.d_input": ["back_qkv_one", "back_qkv_two"],
}


def layer_norm(residual, norm_gain, norm_shift):
    average = jnp.mean(residual, axis=-1, keepdims=True)
    centred = residual - average
    inv_std = lax.rsqrt(jnp.mean(centred * centred, axis=-1, keepdims=True) + EPS)
    normed = centred * inv_std
    return (normed * norm_gain + norm_shift, normed, inv_std)


def norm_back(upstream, normed, inv_std, norm_gain):
    scaled = upstream * norm_gain
    return inv_std * (
        scaled
        - jnp.mean(scaled, axis=-1, keepdims=True)
        - normed * jnp.mean(scaled * normed, axis=-1, keepdims=True)
    )


def gelu_both(v):
    phi_cdf = 0.5 * (1.0 + lax.erf(v * 0.7071067811865476))
    phi_pdf = jnp.exp(-0.5 * v * v) * 0.3989422804014327
    return v * phi_cdf, phi_cdf + v * phi_pdf


def matrix_product(first_op, second_op):
    return jnp.dot(first_op, second_op, preferred_element_type=F32)


def left_t(first_op, second_op):
    return lax.dot_general(
        first_op, second_op, (((0,), (0,)), ((), ())), preferred_element_type=F32
    )


def right_t(first_op, second_op):
    return lax.dot_general(
        first_op, second_op, (((1,), (1,)), ((), ())), preferred_element_type=F32
    )


def column_sum(inputs):
    return jnp.sum(inputs.astype(F32), axis=0)


def n_bits(count):
    return count.bit_length() - 1


class Grid:
    def __init__(self, rows_dev):
        self.n_dp = lax.axis_size("dp")
        self.n_f = lax.axis_size("fsdp")
        self.f_bits = n_bits(self.n_f)
        self.d_bits = n_bits(self.n_dp)
        self.dp = lax.axis_index("dp")
        self.f = lax.axis_index("fsdp")
        self.rows_dev = rows_dev
        self.chips_per_row = self.n_f // (CORES * rows_dev)
        self.members = CORES * self.chips_per_row
        self.core = self.dp % CORES
        self.row_in_group = self.f // self.chips_per_row
        self.member = (self.f % self.chips_per_row) * CORES + self.core

    def my_bit(self, bit):
        if bit < self.f_bits:
            return (self.f >> bit) & 1
        return (self.dp >> (bit - self.f_bits)) & 1

    def swap(self, x, bit):
        if bit < self.f_bits:
            return lax.ppermute(x, "fsdp", [(i, i ^ (1 << bit)) for i in range(self.n_f)])
        flip = 1 << (bit - self.f_bits)
        return lax.ppermute(x, "dp", [(i, i ^ flip) for i in range(self.n_dp)])

    def upper(self, turned):
        bits = list(range(self.f_bits + 1, self.f_bits + self.d_bits))
        return bits if turned else bits[::-1]

    def join(self, own, other, bit, have):
        mine = self.my_bit(bit) == 0
        low = jnp.where(mine, own, other)
        high = jnp.where(mine, other, own)
        return jnp.stack([low, high], axis=sum(1 for b in have if b > bit))

    def gather(self, x, bits):
        out = x
        for n, bit in enumerate(bits):
            other = yield self.swap(out, bit)
            out = self.join(out, other, bit, bits[:n])
        return out.reshape((-1,) + x.shape[1:])

    def gather_two(self, x, y):
        outs = [x, y]
        ways = [self.upper(False), self.upper(True)]
        for n in range(self.d_bits - 1):
            others = yield [self.swap(o, way[n]) for o, way in zip(outs, ways)]
            outs = [
                self.join(o, other, way[n], way[:n])
                for o, other, way in zip(outs, others, ways)
            ]
        core = self.f_bits
        others = yield [self.swap(o, core) for o in outs]
        outs = [self.join(o, other, core, ways[0]) for o, other in zip(outs, others)]
        return [o.reshape((-1,) + v.shape[1:]) for o, v in zip(outs, (x, y))]

    def gather_split(self, x):
        half = x.shape[0] // 2
        outs = [x[:half], x[half:]]
        ways = [self.upper(False), self.upper(True)]
        for n in range(self.d_bits - 1):
            others = yield [self.swap(o, way[n]) for o, way in zip(outs, ways)]
            outs = [
                self.join(o, other, way[n], way[:n])
                for o, other, way in zip(outs, others, ways)
            ]
        out = jnp.concatenate(outs, axis=self.d_bits - 1)
        core = self.f_bits
        other = yield self.swap(out, core)
        return self.join(out, other, core, ways[0]).reshape((-1,) + x.shape[1:])

    def halves(self, x, bit, left):
        place = left.index(bit)
        mine = self.my_bit(bit)
        pick = lambda at: lax.dynamic_index_in_dim(x, at, place, keepdims=False)
        return pick(mine), pick(1 - mine)

    def scatter(self, x, bits):
        left = sorted(bits, reverse=True)
        out = x.reshape((2,) * len(bits) + (-1,) + x.shape[1:])
        for bit in bits:
            kept, sent = self.halves(out, bit, left)
            got = yield self.swap(sent, bit)
            left.remove(bit)
            out = (kept.astype(F32) + got.astype(F32)).astype(BF)
        return out

    def scatter_split(self, x):
        left = list(range(self.f_bits + self.d_bits - 1, self.f_bits - 1, -1))
        out = x.reshape((2,) * self.d_bits + (2, -1) + x.shape[1:])
        kept, sent = self.halves(out, self.f_bits, left)
        got = yield self.swap(sent, self.f_bits)
        out = (kept.astype(F32) + got.astype(F32)).astype(BF)
        left.remove(self.f_bits)
        outs = [lax.index_in_dim(out, h, len(left), keepdims=False) for h in range(2)]
        ways = [self.upper(True), self.upper(False)]
        lefts = [list(left), list(left)]
        for n in range(self.d_bits - 1):
            pairs = [self.halves(o, way[n], l) for o, way, l in zip(outs, ways, lefts)]
            gots = yield [self.swap(sent, way[n]) for (_, sent), way in zip(pairs, ways)]
            outs = [
                (kept.astype(F32) + got.astype(F32)).astype(BF)
                for (kept, _), got in zip(pairs, gots)
            ]
            for l, way in zip(lefts, ways):
                l.remove(way[n])
        return jnp.concatenate(outs, axis=0)

    def source(self, k):
        pairs = []
        for d in range(self.n_dp):
            for f in range(self.n_f):
                base, c = d // CORES * CORES, d % CORES
                b = (f + k) % self.rows_dev
                g = f // self.rows_dev
                row = self.rows_dev * c + b
                target_f = row * self.chips_per_row + g // CORES
                target_d = base + g % CORES
                pairs.append((d * self.n_f + f, target_d * self.n_f + target_f))
        return pairs

    def to_rows(self, x):
        got = []
        for k in range(self.rows_dev):
            block = lax.dynamic_index_in_dim(x, (self.f + k) % self.rows_dev, 0, keepdims=False)
            got.append(lax.ppermute(block, ("dp", "fsdp"), self.source(k)))
        got = yield got
        got = jnp.stack(got)
        b = self.row_in_group % self.rows_dev
        return jnp.concatenate(
            [
                lax.dynamic_index_in_dim(got, (b - p) % self.rows_dev, 0, keepdims=False)
                for p in range(self.rows_dev)
            ]
        )

    def from_rows(self, y):
        parts = y.reshape((self.rows_dev, -1) + y.shape[1:])
        b = self.row_in_group % self.rows_dev
        got = []
        for k in range(self.rows_dev):
            block = lax.dynamic_index_in_dim(parts, (b - k) % self.rows_dev, 0, keepdims=False)
            back = [(t, s) for s, t in self.source(k)]
            got.append(lax.ppermute(block, ("dp", "fsdp"), back))
        got = yield got
        got = jnp.stack(got)
        return jnp.stack(
            [
                lax.dynamic_index_in_dim(got, (row - self.f) % self.rows_dev, 0, keepdims=False)
                for row in range(self.rows_dev)
            ]
        )

    def shift_pairs(self, shift):
        pairs = []
        for d in range(self.n_dp):
            for f in range(self.n_f):
                g = (f % self.chips_per_row) * CORES + d % CORES
                t = (g + shift) % self.members
                td = d // CORES * CORES + t % CORES
                tf = f // self.chips_per_row * self.chips_per_row + t // CORES
                pairs.append((d * self.n_f + f, td * self.n_f + tf))
        return pairs

    def to_member(self, x, shift):
        return lax.ppermute(x, ("dp", "fsdp"), self.shift_pairs(shift))


class Schedule:
    def __init__(self, plan):
        self.plan = plan
        self.makers, self.running, self.waiting, self.result = {}, {}, {}, {}

    def add(self, name, maker, *operands):
        self.makers[name] = (maker, operands)

    def step(self, name, value):
        try:
            self.waiting[name] = (
                next(self.running[name]) if value is None else self.running[name].send(value)
            )
        except StopIteration as end:
            self.waiting.pop(name, None)
            self.result[name] = end.value

    def tick(self, point, value):
        names = [n for n in self.plan.get(point, ()) if n not in self.result]
        if not names:
            return value
        arrived = {n: self.waiting[n] for n in names if n in self.running}
        fresh = {n: self.makers[n][1] for n in names if n not in self.running}
        value, arrived, fresh = lax.optimization_barrier((value, arrived, fresh))
        for name in names:
            if name in arrived:
                self.step(name, arrived[name])
            else:
                self.running[name] = self.makers[name][0](*fresh[name])
                self.step(name, None)
        return value

    def get(self, name):
        return self.finish(name)[0]

    def finish(self, *names):
        while any(n not in self.result for n in names):
            for name in names:
                if name not in self.running:
                    self.running[name] = self.makers[name][0](*self.makers[name][1])
                    self.step(name, None)
                elif name not in self.result:
                    self.step(name, self.waiting[name])
        return [self.result[n] for n in names]


def dot_nt(a, b):
    return lax.dot_general(a, b, (((1,), (1,)), ((), ())), preferred_element_type=F32)


def dot_nn(a, b):
    return lax.dot_general(a, b, (((1,), (0,)), ((), ())), preferred_element_type=F32)


def dot_tn(a, b):
    return lax.dot_general(a, b, (((0,), (0,)), ((), ())), preferred_element_type=F32)


def head_only(x, head):
    lane = lax.broadcasted_iota(jnp.int32, x.shape, 1)
    keep = (lane >= HEAD_DIM) if head else (lane < HEAD_DIM)
    return jnp.where(keep, x, jnp.zeros_like(x))


def attend_kernel(chunks, q_step, *refs):
    q_ref = refs[0]
    k_refs = refs[1 : 1 + chunks]
    v_refs = refs[1 + chunks : 1 + 2 * chunks]
    seg_q_ref, seg_k_ref, o_ref, lse_ref = refs[1 + 2 * chunks :]
    tokens = q_ref.shape[0]
    for q0 in range(0, tokens, q_step):
        q = q_ref[q0 : q0 + q_step, :]
        seg_q = seg_q_ref[:, q0 : q0 + q_step]
        halves = []
        for head in range(2):
            q_head = head_only(q, head)
            scores = []
            for c in range(chunks):
                s = dot_nt(k_refs[c][...], q_head) * SCALING
                seg_k = seg_k_ref[c * tokens : (c + 1) * tokens, :]
                scores.append(jnp.where(seg_k == seg_q, s, NEGATIVE))
            highest = functools.reduce(
                jnp.maximum, [jnp.max(s, axis=0, keepdims=True) for s in scores]
            )
            powers = [jnp.exp(s - highest) for s in scores]
            total = functools.reduce(
                jnp.add, [jnp.sum(p, axis=0, keepdims=True) for p in powers]
            )
            inverse = 1.0 / total
            mixed = functools.reduce(
                jnp.add,
                [dot_tn(v_refs[c][...], (powers[c] * inverse).astype(BF)) for c in range(chunks)],
            )
            halves.append(mixed[head * HEAD_DIM : (head + 1) * HEAD_DIM, :])
            lse_ref[0, head : head + 1, q0 : q0 + q_step] = highest + jnp.log(total)
        both = jnp.concatenate(halves, axis=0)
        o_ref[q0 : q0 + q_step, :] = both.T.astype(BF)


def attend_back_kernel(chunks, q_step, *refs):
    q_ref = refs[0]
    k_refs = refs[1 : 1 + chunks]
    v_refs = refs[1 + chunks : 1 + 2 * chunks]
    do_ref, lse_ref, seg_q_ref, seg_k_ref = refs[1 + 2 * chunks : 5 + 2 * chunks]
    dq_ref, own_ref = refs[5 + 2 * chunks : 7 + 2 * chunks]
    other_refs = refs[7 + 2 * chunks : 6 + 3 * chunks]
    acc_ref = refs[6 + 3 * chunks]
    tokens = q_ref.shape[0]
    first = True
    for q0 in range(0, tokens, q_step):
        q = q_ref[q0 : q0 + q_step, :]
        do = do_ref[q0 : q0 + q_step, :]
        seg_q = seg_q_ref[:, q0 : q0 + q_step]
        halves = []
        for head in range(2):
            q_head = head_only(q, head)
            do_head = head_only(do, head)
            lse = lse_ref[0, head : head + 1, q0 : q0 + q_step]
            probs, d_probs = [], []
            for c in range(chunks):
                s = dot_nt(k_refs[c][...], q_head) * SCALING
                seg_k = seg_k_ref[c * tokens : (c + 1) * tokens, :]
                s = jnp.where(seg_k == seg_q, s, NEGATIVE)
                probs.append(jnp.exp(s - lse))
                d_probs.append(dot_nt(v_refs[c][...], do_head))
            offset = functools.reduce(
                jnp.add,
                [jnp.sum(p * d, axis=0, keepdims=True) for p, d in zip(probs, d_probs)],
            )
            dq_t = None
            for c in range(chunks):
                ds = (probs[c] * (d_probs[c] - offset)).astype(BF)
                dk = dot_nn(ds, q_head) * SCALING
                dv = dot_nn(probs[c].astype(BF), do_head)
                term = dot_tn(k_refs[c][...], ds)
                dq_t = term if dq_t is None else dq_t + term
                if first:
                    acc_ref[c, 0] = dk
                    acc_ref[c, 1] = dv
                else:
                    acc_ref[c, 0] += dk
                    acc_ref[c, 1] += dv
            first = False
            halves.append(dq_t[head * HEAD_DIM : (head + 1) * HEAD_DIM, :])
        both = jnp.concatenate(halves, axis=0) * SCALING
        dq_ref[q0 : q0 + q_step, :] = both.T.astype(BF)
    own_ref[...] = acc_ref[0]
    for c in range(1, chunks):
        other_refs[c - 1][...] = acc_ref[c].astype(BF)


def attention_specs(qkv, others):
    tokens = qkv.shape[0]
    pairs = HEADS // 2
    block = (tokens, PAIR)
    at = lambda offset: pl.BlockSpec(block, lambda i, offset=offset: (0, offset + i))
    operands = [qkv, qkv] + others + [qkv] + others
    specs = (
        [at(0), at(pairs)]
        + [at(0) for _ in others]
        + [at(2 * pairs)]
        + [at(pairs) for _ in others]
    )
    return operands, specs, tokens, pairs


def attend(qkv, others, seg_q, seg_k):
    operands, specs, tokens, pairs = attention_specs(qkv, others)
    chunks = 1 + len(others)
    length = tokens * chunks
    whole = lambda shape: pl.BlockSpec(shape, lambda i: (0,) * len(shape))
    return pl.pallas_call(
        functools.partial(attend_kernel, chunks, min(256, tokens)),
        grid=(pairs,),
        in_specs=specs + [whole((1, tokens)), whole((length, 1))],
        out_specs=[
            pl.BlockSpec((tokens, PAIR), lambda i: (0, i)),
            pl.BlockSpec((1, 2, tokens), lambda i: (i, 0, 0)),
        ],
        out_shape=[
            jax.ShapeDtypeStruct((tokens, HEADS * HEAD_DIM), BF),
            jax.ShapeDtypeStruct((pairs, 2, tokens), F32),
        ],
        compiler_params=pltpu.CompilerParams(vmem_limit_bytes=40 * 2**20),
        cost_estimate=pl.CostEstimate(
            flops=16 * tokens * length * HEADS * HEAD_DIM,
            bytes_accessed=8 * length * HEADS * HEAD_DIM,
            transcendentals=tokens * length * HEADS,
        ),
        name="attend",
    )(*operands, seg_q, seg_k)


def attend_back(qkv, others, d_mixture, lse, seg_q, seg_k):
    operands, specs, tokens, pairs = attention_specs(qkv, others)
    chunks = 1 + len(others)
    length = tokens * chunks
    width = HEADS * HEAD_DIM
    whole = lambda shape: pl.BlockSpec(shape, lambda i: (0,) * len(shape))
    stacked = pl.BlockSpec((2, tokens, PAIR), lambda i: (0, 0, i))
    out = pl.pallas_call(
        functools.partial(attend_back_kernel, chunks, min(256, tokens)),
        grid=(pairs,),
        in_specs=specs
        + [
            pl.BlockSpec((tokens, PAIR), lambda i: (0, i)),
            pl.BlockSpec((1, 2, tokens), lambda i: (i, 0, 0)),
            whole((1, tokens)),
            whole((length, 1)),
        ],
        out_specs=[pl.BlockSpec((tokens, PAIR), lambda i: (0, i)), stacked]
        + [stacked for _ in others],
        out_shape=[
            jax.ShapeDtypeStruct((tokens, width), BF),
            jax.ShapeDtypeStruct((2, tokens, width), F32),
        ]
        + [jax.ShapeDtypeStruct((2, tokens, width), BF) for _ in others],
        scratch_shapes=[pltpu.VMEM((chunks, 2, tokens, PAIR), F32)],
        compiler_params=pltpu.CompilerParams(vmem_limit_bytes=40 * 2**20),
        cost_estimate=pl.CostEstimate(
            flops=40 * tokens * length * width,
            bytes_accessed=20 * length * width,
            transcendentals=tokens * length * HEADS,
        ),
        name="attend_back",
    )(*operands, d_mixture, lse, seg_q, seg_k)
    return out[0], out[1], out[2:]


def split_small(small, sizes):
    vectors, at = [], 0
    for size in sizes:
        vectors.append(small[:, at : at + size].reshape(-1).astype(F32))
        at += size
    return vectors


def layer_forward(grid, tag, tick, inputs, weights, seg_q, seg_k):
    width = inputs.shape[1]
    x_low = inputs.astype(BF)
    qkv_w, attn_w, qv_b, attn_b, attn_g, attn_s, inner_b, outer_b, ffn_g, ffn_s = weights("qkv")
    bias = jnp.concatenate([qv_b[:width], jnp.zeros((width,), F32), qv_b[width:]])
    qkv = (matrix_product(x_low, qkv_w) + bias).astype(BF)
    qkv = tick(tag + "qkv", qkv)
    key_value = qkv[:, width:]
    others = [grid.to_member(key_value, shift) for shift in range(1, grid.members)]
    mixture, lse = attend(qkv, others, seg_q, seg_k)
    mixture = tick(tag + "attend", mixture)
    branch = matrix_product(mixture, attn_w) + attn_b
    normed, normed_one, inv_one = layer_norm(inputs.astype(F32) + branch, attn_g, attn_s)
    normed = tick(tag + "normed", normed)
    inner_w, outer_w = weights("ffn")
    normed_low = normed.astype(BF)
    inner = matrix_product(normed_low, inner_w) + inner_b
    active, slope = gelu_both(inner)
    active = tick(tag + "active", active.astype(BF))
    outer = matrix_product(active, outer_w) + outer_b
    output, normed_two, inv_two = layer_norm(normed + outer, ffn_g, ffn_s)
    output = tick(tag + "out", output)
    saved = (x_low, qkv, others, lse, mixture, normed_one, inv_one, normed_low, slope, active, normed_two, inv_two)
    return output, saved


def layer_backward(grid, tag, tick, give, upstream, weights, saved, seg_q, seg_k):
    qkv_w, attn_w, qv_b, attn_b, attn_g, attn_s, inner_b, outer_b, ffn_g, ffn_s = weights("qkv")
    inner_w, outer_w = weights("ffn")
    (x_low, qkv, others, lse, mixture, normed_one, inv_one, normed_low, slope, active, normed_two, inv_two) = saved
    grad_ffn_g = jnp.sum(upstream * normed_two, axis=0)
    grad_ffn_s = jnp.sum(upstream, axis=0)
    d_second = norm_back(upstream, normed_two, inv_two, ffn_g)
    d_outer = d_second.astype(BF)
    grad_outer_b = column_sum(d_outer)
    grad_outer_w = left_t(active, d_outer).astype(BF)
    give("outer", grad_outer_w)
    d_outer, grad_outer_w = lax.optimization_barrier((d_outer, grad_outer_w))
    d_outer = tick(tag + "d_outer", d_outer)
    d_inner = (right_t(d_outer, outer_w) * slope).astype(BF)
    grad_inner_b = column_sum(d_inner)
    grad_inner_w = left_t(normed_low, d_inner).astype(BF)
    give("inner", grad_inner_w)
    d_inner, grad_inner_w = lax.optimization_barrier((d_inner, grad_inner_w))
    d_inner = tick(tag + "d_inner", d_inner)
    d_normed = right_t(d_inner, inner_w) + d_second
    grad_attn_g = jnp.sum(d_normed * normed_one, axis=0)
    grad_attn_s = jnp.sum(d_normed, axis=0)
    d_first = norm_back(d_normed, normed_one, inv_one, attn_g)
    d_branch = d_first.astype(BF)
    grad_attn_b = column_sum(d_branch)
    grad_attn_w = left_t(mixture, d_branch).astype(BF)
    d_mixture = right_t(d_branch, attn_w).astype(BF)
    d_mixture = tick(tag + "d_mixture", d_mixture)
    d_queries, own, for_others = attend_back(qkv, others, d_mixture, lse, seg_q, seg_k)
    d_queries = tick(tag + "d_queries", d_queries)
    for shift in range(1, grid.members):
        own = own + grid.to_member(for_others[shift - 1], -shift).astype(F32)
    own = own.astype(BF)
    d_qkv = jnp.concatenate([d_queries, own[0], own[1]], axis=1)
    grad_qv_b = jnp.concatenate([column_sum(d_queries), column_sum(own[1])])
    grad_qkv_w = left_t(x_low, d_qkv).astype(BF)
    small = (grad_qv_b, grad_attn_b, grad_attn_g, grad_attn_s, grad_inner_b, grad_outer_b, grad_ffn_g, grad_ffn_s)
    give("qkv", grad_qkv_w, grad_attn_w, small)
    d_qkv = tick(tag + "d_qkv", d_qkv)
    d_input = right_t(d_qkv, qkv_w) + d_first
    d_input = tick(tag + "d_input", d_input)
    return d_input


def contrastive(vectors, positives):
    count, width = vectors.shape
    similarity = jnp.dot(vectors, vectors.T, precision=FULL_PRECISION) / (width * SOFTMAX_HEAT)
    ids = jnp.arange(count, dtype=jnp.int32)
    similarity = jnp.where(ids[:, None] == ids[None, :], NEGATIVE, similarity)
    highest = jnp.max(similarity, axis=1, keepdims=True)
    totals = highest + jnp.log(jnp.sum(jnp.exp(similarity - highest), axis=1, keepdims=True))
    positive = positives[:, None] == ids[None, :]
    loss = jnp.sum(totals) - jnp.sum(jnp.where(positive, similarity, 0.0))
    slope = (jnp.exp(similarity - totals) - positive.astype(F32)) / (width * SOFTMAX_HEAT)
    return loss, jnp.dot(slope + slope.T, vectors, precision=FULL_PRECISION)


def body(
    hidden,
    skip_tokens,
    backbone_cotangent,
    head_cotangent,
    starts,
    positives,
    qkv_weight,
    qv_bias,
    attn_weight,
    attn_bias,
    attn_gain,
    attn_shift,
    inner_weight,
    inner_bias,
    outer_weight,
    outer_bias,
    ffn_gain,
    ffn_shift,
):
    rows_dev, local, width = hidden.shape
    grid = Grid(rows_dev)
    tokens = rows_dev * local
    length = tokens * grid.members

    starts_both = jnp.stack([starts, grid.swap(starts, grid.f_bits)])
    from_other = jnp.where(grid.row_in_group // rows_dev == grid.core, 0, 1)
    my_starts = lax.dynamic_index_in_dim(starts_both, from_other, 0, keepdims=False)
    my_starts = lax.dynamic_index_in_dim(
        my_starts, grid.row_in_group % rows_dev, 0, keepdims=False
    )
    place = jnp.arange(tokens, dtype=jnp.int32)
    q_pos = grid.member * tokens + place
    k_pos = jnp.concatenate(
        [
            (grid.member - shift) % grid.members * tokens + place
            for shift in range(grid.members)
        ]
    )
    segment = lambda pos: jnp.sum((my_starts[:, None] <= pos[None, :]).astype(jnp.int32), axis=0) - 1
    seg_q = segment(q_pos)[None, :]
    seg_k = segment(k_pos)[:, None]
    cls_hot = (my_starts[:, None] == q_pos[None, :]).astype(F32)
    is_cls = jnp.any(my_starts[:, None] == q_pos[None, :], axis=0)[:, None]

    devices = grid.n_dp * grid.n_f
    z_up, z_down = list(range(grid.f_bits)), list(range(grid.f_bits))[::-1]
    vectors = (qv_bias, attn_bias, attn_gain, attn_shift, inner_bias, outer_bias, ffn_gain, ffn_shift)
    sizes = [v.shape[1] for v in vectors]
    rows = qkv_weight.shape[1]
    small_own = jnp.concatenate(vectors, axis=1).reshape(rows, -1)
    small_cols = small_own.shape[1]
    padded = -(-small_cols // 128) * 128
    small_own = jnp.pad(small_own, ((0, 0), (0, padded - small_cols)))
    schedule = Schedule(PLAN)
    tick = schedule.tick

    def gather_qkv(*parts):
        out = jnp.concatenate(parts, axis=1)
        out = yield from grid.gather(out, z_up)
        return (yield from grid.gather_split(out))

    def gather_ffn(inner, outer):
        deep = outer.shape[0] // inner.shape[0]
        out = jnp.concatenate([inner, outer.reshape(inner.shape[0], -1)], axis=1)
        out = yield from grid.gather(out, z_up)
        inner, outer = out[:, : inner.shape[1]], out[:, inner.shape[1] :]
        return (yield from grid.gather_two(inner, outer.reshape(inner.shape[0] * deep, -1)))

    for layer, tag in ((0, "one"), (1, "two")):
        parts = [qkv_weight[layer], attn_weight[layer]] + ([small_own] if layer == 0 else [])
        schedule.add("qkv_" + tag, gather_qkv, *parts)
        schedule.add("ffn_" + tag, gather_ffn, inner_weight[layer], outer_weight[layer])
    schedule.add("hidden", grid.to_rows, hidden)
    schedule.add("skip", grid.to_rows, skip_tokens)
    schedule.add("cots", grid.to_rows, jnp.concatenate([head_cotangent, backbone_cotangent], axis=2))

    small = []

    def weights_of(layer, tag):
        def get(which):
            if which == "ffn":
                return schedule.get("ffn_" + tag)
            if not small:
                every = schedule.get("qkv_one")[:, -padded:][:, :small_cols]
                small.append(every.reshape(devices, 2, -1))
            pack = schedule.get("qkv_" + tag)
            cut = qkv_weight.shape[2]
            return (pack[:, :cut], pack[:, cut : cut + width], *split_small(small[0][:, layer], sizes))

        return get

    def scatter_qkv(*parts):
        out = jnp.concatenate(parts, axis=1)
        out = yield from grid.scatter_split(out)
        return (yield from grid.scatter(out, z_down))

    core_first = lambda turned: [grid.f_bits] + grid.upper(turned)

    def scatter_z(inner, outer):
        deep = outer.shape[0] // inner.shape[0]
        out = jnp.concatenate([inner, outer.reshape(inner.shape[0], -1)], axis=1)
        out = yield from grid.scatter(out, z_down)
        return out[:, : inner.shape[1]], out[:, inner.shape[1] :].reshape(out.shape[0] * deep, -1)

    kept_small = {}

    def give_to(tag):
        def give(which, *grads):
            if which == "qkv":
                *grads, vectors = grads
                kept_small[tag] = vectors
                if tag == "one":
                    cut = [
                        jnp.concatenate([v.reshape(devices, -1) for v in kept_small[t]], axis=1)
                        for t in ("one", "two")
                    ]
                    flat = jnp.stack(cut, axis=1).reshape(devices * rows, small_cols).astype(BF)
                    grads.append(jnp.pad(flat, ((0, 0), (0, padded - small_cols))))
                schedule.add("back_qkv_" + tag, scatter_qkv, *grads)
            else:
                turned = which == "inner"
                schedule.add(
                    "back_" + which + "_" + tag,
                    lambda g: grid.scatter(g, core_first(turned)),
                    grads[0],
                )

        return give

    def z_of(tag):
        schedule.add(
            "back_z_" + tag,
            scatter_z,
            schedule.get("back_inner_" + tag),
            schedule.get("back_outer_" + tag),
        )

    mark = jnp.zeros((8, 128), F32) + my_starts[0].astype(F32)
    for n in range(GATHER_TICKS):
        mark = tick("g%d" % n, mark)
    x = schedule.get("hidden")
    first, saved_one = layer_forward(grid, "f0.", tick, x, weights_of(0, "one"), seg_q, seg_k)

    shared = n_bits(grid.chips_per_row)
    cls_bits = list(range(shared, grid.f_bits)) + grid.upper(True)

    def gather_cls(own):
        for bit in [grid.f_bits] + list(range(shared)):
            got = yield grid.swap(own, bit)
            own = own + got
        return (yield from grid.gather(own, cls_bits))

    schedule.add("cls", gather_cls, jnp.dot(cls_hot, first, precision=FULL_PRECISION)[None])
    for n in range(HEAD_TICKS):
        first = tick("h%d" % n, first)
    head_in = jnp.where(is_cls, first, schedule.get("skip").astype(F32))
    second, saved_two = layer_forward(grid, "f1.", tick, head_in, weights_of(1, "two"), seg_q, seg_k)

    cots = schedule.get("cots")
    schedule.add(
        "outs", grid.from_rows, jnp.concatenate([first.astype(BF), second.astype(BF)], axis=1)
    )
    head_up = tick("t", cots[:, :width]).astype(F32)
    d_head_in = layer_backward(
        grid, "b1.", tick, give_to("two"), head_up, weights_of(1, "two"), saved_two, seg_q, seg_k
    )
    [cls_all] = schedule.finish("cls")
    contrast_loss, d_cls_all = contrastive(cls_all.reshape(-1, width), positives)
    my_row = grid.dp // CORES * (CORES * rows_dev) + grid.row_in_group
    d_cls = lax.dynamic_slice_in_dim(d_cls_all, my_row * SEGS, SEGS, 0)
    upstream = (
        cots[:, width:].astype(F32)
        + jnp.where(is_cls, d_head_in, 0.0)
        + lax.dot_general(cls_hot, d_cls, (((0,), (0,)), ((), ())), precision=FULL_PRECISION)
    )
    schedule.add("skip_back", grid.from_rows, jnp.where(is_cls, 0.0, d_head_in).astype(BF))
    z_of("two")
    upstream = tick("u", upstream)
    d_input = layer_backward(
        grid, "b0.", tick, give_to("one"), upstream, weights_of(0, "one"), saved_one, seg_q, seg_k
    )
    schedule.add("hidden_back", grid.from_rows, d_input.astype(BF))
    schedule.finish("back_inner_one", "back_outer_one")
    z_of("one")
    mark = jnp.zeros((8, 128), F32)
    for n in range(TAIL_TICKS):
        mark = tick("e%d" % n, mark)
    names = ["hidden_back", "skip_back", "outs", "back_z_one", "back_z_two", "back_qkv_one", "back_qkv_two"]
    hidden_back, skip_back, outs, (inner_1, outer_1), (inner_2, outer_2), qkv_1, qkv_2 = schedule.finish(*names)

    cut = qkv_weight.shape[2]
    pair = lambda a, b: jnp.stack([a, b]).astype(F32)
    small_g = qkv_1[:, -padded:][:, :small_cols].reshape(2, -1).astype(F32)
    cuts, at = [], 0
    for size in sizes:
        cuts.append(small_g[:, at : at + size])
        at += size
    return (
        contrast_loss,
        outs[:, :, :width],
        outs[:, :, width:],
        hidden_back.astype(F32),
        skip_back.astype(F32),
        pair(qkv_1[:, :cut], qkv_2[:, :cut]),
        cuts[0],
        pair(qkv_1[:, cut : cut + width], qkv_2[:, cut : cut + width]),
        cuts[1],
        cuts[2],
        cuts[3],
        pair(inner_1, inner_2),
        cuts[4],
        pair(outer_1, outer_2),
        cuts[5],
        cuts[6],
        cuts[7],
    )


def solution(mesh):
    rows = P("dp", "fsdp", None)
    matrix = P(None, ("dp", "fsdp"), None)
    vector = P(None, ("dp", "fsdp"))
    params = (
        matrix,
        vector,
        matrix,
        vector,
        vector,
        vector,
        matrix,
        vector,
        matrix,
        vector,
        vector,
        vector,
    )
    return jax.shard_map(
        body,
        mesh=mesh,
        in_specs=(rows, rows, rows, rows, P("dp", None), P()) + params,
        out_specs=(P(), rows, rows, rows, rows) + params,
        check_vma=False,
    )
```

```python
import functools

import jax
import jax.numpy as jnp
from jax import lax
from jax.experimental import pallas as pl
from jax.experimental.pallas import tpu as pltpu
from jax.sharding import PartitionSpec as P

HEADS = 12
HEAD_DIM = 64
SEGS = 8
CORES = 2

EPS = 1e-12
SOFTMAX_HEAT = 0.02
NEGATIVE = -1e30
FULL_PRECISION = lax.Precision.HIGHEST
SCALING = HEAD_DIM ** (-0.5)
PAIR = 2 * HEAD_DIM
BF = jnp.bfloat16
F32 = jnp.float32

(
    QKV_1, FFN_1, QKV_2, FFN_2, HIDDEN, SKIP, COTS, CLS, OUTS, SKIP_BACK, HIDDEN_BACK,
    OUTER_G1, INNER_G1, FFN_G1, QKV_G1, OUTER_G2, INNER_G2, FFN_G2, QKV_G2,
) = range(19)
START, F0, BETWEEN, F1, TURN, B1, UP, B0, END = range(9)
AT_QKV, AT_HALF, AT_MIX, AT_NORM, AT_FFN, AT_ACTIVE, AT_OUT = range(7)
AT_D_OUTER, AT_D_INNER, AT_D_NORM, AT_D_MIX, AT_D_HALF, AT_D_QUERY, AT_D_QKV, AT_D_INPUT = range(8)
START_TICKS, BETWEEN_TICKS, END_TICKS = 7, 1, 4
LATE = (FFN_G1, FFN_G2)
PLAN = {
    (START, 0): [QKV_1],
    (START, 1): [QKV_1, FFN_1],
    (START, 2): [QKV_1, FFN_1],
    (START, 3): [QKV_1, FFN_1],
    (START, 4): [QKV_1, HIDDEN],
    (START, 5): [QKV_1, FFN_1],
    (START, 6): [QKV_1, HIDDEN, QKV_2],
    (F0, AT_QKV): [FFN_1, QKV_2, FFN_2],
    (F0, AT_HALF): [QKV_2, FFN_2],
    (F0, AT_MIX): [FFN_1, QKV_2, FFN_2],
    (F0, AT_NORM): [FFN_1, QKV_2, SKIP],
    (F0, AT_OUT): [QKV_2, FFN_2, CLS],
    (BETWEEN, 0): [QKV_2, SKIP, CLS],
    (F1, AT_QKV): [FFN_2, CLS],
    (F1, AT_HALF): [CLS],
    (F1, AT_MIX): [FFN_2, CLS],
    (F1, AT_NORM): [FFN_2, CLS],
    (TURN, 0): [OUTS],
    (B1, AT_D_OUTER): [OUTER_G2],
    (B1, AT_D_INNER): [OUTER_G2, INNER_G2],
    (B1, AT_D_MIX): [INNER_G2, OUTS],
    (B1, AT_D_HALF): [OUTER_G2, COTS],
    (B1, AT_D_QUERY): [INNER_G2],
    (B1, AT_D_QKV): [OUTER_G2, INNER_G2, FFN_G2, QKV_G2, COTS],
    (UP, 0): [FFN_G2, QKV_G2, SKIP_BACK],
    (B0, AT_D_OUTER): [OUTER_G1],
    (B0, AT_D_INNER): [FFN_G2, QKV_G2, OUTER_G1, INNER_G1],
    (B0, AT_D_MIX): [FFN_G2, INNER_G1],
    (B0, AT_D_HALF): [QKV_G2, OUTER_G1],
    (B0, AT_D_QUERY): [INNER_G1, QKV_G2, SKIP_BACK],
    (B0, AT_D_QKV): [OUTER_G1, INNER_G1, QKV_G1, FFN_G1, QKV_G2],
    (B0, AT_D_INPUT): [QKV_G1, HIDDEN_BACK, FFN_G1, QKV_G2],
    (END, 0): [QKV_G1, FFN_G1],
    (END, 1): [QKV_G1],
    (END, 2): [QKV_G1, HIDDEN_BACK, FFN_G1],
    (END, 3): [QKV_G1],
}


def layer_norm(residual, norm_gain, norm_shift):
    average = jnp.mean(residual, axis=-1, keepdims=True)
    centred = residual - average
    inv_std = lax.rsqrt(jnp.mean(centred * centred, axis=-1, keepdims=True) + EPS)
    normed = centred * inv_std
    return (normed * norm_gain + norm_shift, normed, inv_std)


def norm_back(upstream, normed, inv_std, norm_gain):
    scaled = upstream * norm_gain
    return inv_std * (
        scaled
        - jnp.mean(scaled, axis=-1, keepdims=True)
        - normed * jnp.mean(scaled * normed, axis=-1, keepdims=True)
    )


def gelu_both(v):
    phi_cdf = 0.5 * (1.0 + lax.erf(v * 0.7071067811865476))
    phi_pdf = jnp.exp(-0.5 * v * v) * 0.3989422804014327
    return v * phi_cdf, phi_cdf + v * phi_pdf


def matrix_product(first_op, second_op):
    return jnp.dot(first_op, second_op, preferred_element_type=F32)


def left_t(first_op, second_op):
    return lax.dot_general(
        first_op, second_op, (((0,), (0,)), ((), ())), preferred_element_type=F32
    )


def right_t(first_op, second_op):
    return lax.dot_general(
        first_op, second_op, (((1,), (1,)), ((), ())), preferred_element_type=F32
    )


def column_sum(inputs):
    return jnp.sum(inputs.astype(F32), axis=0)


def n_bits(count):
    return count.bit_length() - 1


class Grid:
    def __init__(self, rows_dev):
        self.n_dp = lax.axis_size("dp")
        self.n_f = lax.axis_size("fsdp")
        self.f_bits = n_bits(self.n_f)
        self.d_bits = n_bits(self.n_dp)
        self.dp = lax.axis_index("dp")
        self.f = lax.axis_index("fsdp")
        self.rows_dev = rows_dev
        self.chips_per_row = self.n_f // (CORES * rows_dev)
        self.members = CORES * self.chips_per_row
        self.core = self.dp % CORES
        self.row_in_group = self.f // self.chips_per_row
        self.member = (self.f % self.chips_per_row) * CORES + self.core

    def my_bit(self, bit):
        if bit < self.f_bits:
            return (self.f >> bit) & 1
        return (self.dp >> (bit - self.f_bits)) & 1

    def swap(self, x, bit):
        if bit < self.f_bits:
            return lax.ppermute(x, "fsdp", [(i, i ^ (1 << bit)) for i in range(self.n_f)])
        flip = 1 << (bit - self.f_bits)
        return lax.ppermute(x, "dp", [(i, i ^ flip) for i in range(self.n_dp)])

    def upper(self, turned):
        bits = list(range(self.f_bits + 1, self.f_bits + self.d_bits))
        return bits if turned else bits[::-1]

    def join(self, own, other, bit, have):
        place = sum(1 for b in have if b > bit)
        mine = self.my_bit(bit) == 0
        low = jnp.where(mine, own, other)
        high = jnp.where(mine, other, own)
        return lax.optimization_barrier(jnp.stack([low, high], axis=place))

    def gather(self, x, bits):
        out = x
        for n, bit in enumerate(bits):
            other = yield self.swap(out, bit)
            out = self.join(out, other, bit, bits[:n])
        return out.reshape((-1,) + x.shape[1:])

    def gather_z(self, x):
        if self.n_f != 4:
            return (yield from self.gather(x, list(range(self.f_bits))))
        other = yield self.swap(x, 0)
        pair = self.join(x, other, 0, [])
        middle = yield lax.ppermute(pair, "fsdp", [(1, 2), (2, 1)])
        outer = yield lax.ppermute(middle, "fsdp", [(1, 0), (2, 3)])
        inside = (self.f == 1) | (self.f == 2)
        out = self.join(pair, jnp.where(inside, middle, outer), 1, [0])
        return out.reshape((-1,) + x.shape[1:])

    def scatter_z(self, x):
        if self.n_f != 4:
            return (yield from self.scatter(x, list(range(self.f_bits))[::-1]))
        out = x.reshape((2, 2, -1) + x.shape[1:])
        kept, sent = self.halves(out, 1, [1, 0])
        inward = yield lax.ppermute(sent, "fsdp", [(0, 1), (3, 2)])
        summed = (sent.astype(F32) + inward.astype(F32)).astype(BF)
        middle = yield lax.ppermute(summed, "fsdp", [(1, 2), (2, 1)])
        out = (kept.astype(F32) + middle.astype(F32)).astype(BF)
        kept, sent = self.halves(out, 0, [0])
        got = yield self.swap(sent, 0)
        return (kept.astype(F32) + got.astype(F32)).astype(BF)

    def gather_two(self, x, y):
        outs = [x, y]
        ways = [self.upper(False), self.upper(True)]
        for n in range(self.d_bits - 1):
            others = yield [self.swap(o, way[n]) for o, way in zip(outs, ways)]
            outs = [
                self.join(o, other, way[n], way[:n])
                for o, other, way in zip(outs, others, ways)
            ]
        core = self.f_bits
        others = yield [self.swap(o, core) for o in outs]
        outs = [self.join(o, other, core, ways[0]) for o, other in zip(outs, others)]
        return [o.reshape((-1,) + v.shape[1:]) for o, v in zip(outs, (x, y))]

    def gather_split(self, x):
        half = x.shape[0] // 2
        outs = [x[:half], x[half:]]
        ways = [self.upper(False), self.upper(True)]
        for n in range(self.d_bits - 1):
            others = yield [self.swap(o, way[n]) for o, way in zip(outs, ways)]
            outs = [
                self.join(o, other, way[n], way[:n])
                for o, other, way in zip(outs, others, ways)
            ]
        out = jnp.concatenate(outs, axis=self.d_bits - 1)
        core = self.f_bits
        other = yield self.swap(out, core)
        return self.join(out, other, core, ways[0]).reshape((-1,) + x.shape[1:])

    def halves(self, x, bit, left):
        place = left.index(bit)
        mine = self.my_bit(bit)
        pick = lambda at: lax.dynamic_index_in_dim(x, at, place, keepdims=False)
        return pick(mine), pick(1 - mine)

    def scatter(self, x, bits):
        left = sorted(bits, reverse=True)
        out = x.reshape((2,) * len(bits) + (-1,) + x.shape[1:])
        for bit in bits:
            kept, sent = self.halves(out, bit, left)
            got = yield self.swap(sent, bit)
            left.remove(bit)
            out = (kept.astype(F32) + got.astype(F32)).astype(BF)
        return out

    def scatter_split(self, x):
        left = list(range(self.f_bits + self.d_bits - 1, self.f_bits - 1, -1))
        out = x.reshape((2,) * self.d_bits + (2, -1) + x.shape[1:])
        kept, sent = self.halves(out, self.f_bits, left)
        got = yield self.swap(sent, self.f_bits)
        out = (kept.astype(F32) + got.astype(F32)).astype(BF)
        left.remove(self.f_bits)
        outs = [lax.index_in_dim(out, h, len(left), keepdims=False) for h in range(2)]
        ways = [self.upper(True), self.upper(False)]
        lefts = [list(left), list(left)]
        for n in range(self.d_bits - 1):
            pairs = [self.halves(o, way[n], l) for o, way, l in zip(outs, ways, lefts)]
            gots = yield [self.swap(sent, way[n]) for (_, sent), way in zip(pairs, ways)]
            outs = [
                (kept.astype(F32) + got.astype(F32)).astype(BF)
                for (kept, _), got in zip(pairs, gots)
            ]
            for l, way in zip(lefts, ways):
                l.remove(way[n])
        return jnp.concatenate(outs, axis=0)

    def source(self, k):
        pairs = []
        for d in range(self.n_dp):
            for f in range(self.n_f):
                base, c = d // CORES * CORES, d % CORES
                b = (f + k) % self.rows_dev
                g = f // self.rows_dev
                row = self.rows_dev * c + b
                target_f = row * self.chips_per_row + g // CORES
                target_d = base + g % CORES
                pairs.append((d * self.n_f + f, target_d * self.n_f + target_f))
        return pairs

    def to_rows(self, x):
        got = []
        for k in range(self.rows_dev):
            block = lax.dynamic_index_in_dim(x, (self.f + k) % self.rows_dev, 0, keepdims=False)
            got.append(lax.ppermute(block, ("dp", "fsdp"), self.source(k)))
        got = yield got
        got = jnp.stack(got)
        b = self.row_in_group % self.rows_dev
        return jnp.concatenate(
            [
                lax.dynamic_index_in_dim(got, (b - p) % self.rows_dev, 0, keepdims=False)
                for p in range(self.rows_dev)
            ]
        )

    def from_rows(self, y):
        parts = y.reshape((self.rows_dev, -1) + y.shape[1:])
        b = self.row_in_group % self.rows_dev
        got = []
        for k in range(self.rows_dev):
            block = lax.dynamic_index_in_dim(parts, (b - k) % self.rows_dev, 0, keepdims=False)
            back = [(t, s) for s, t in self.source(k)]
            got.append(lax.ppermute(block, ("dp", "fsdp"), back))
        got = yield got
        got = jnp.stack(got)
        return jnp.stack(
            [
                lax.dynamic_index_in_dim(got, (row - self.f) % self.rows_dev, 0, keepdims=False)
                for row in range(self.rows_dev)
            ]
        )

    def shift_pairs(self, shift):
        pairs = []
        for d in range(self.n_dp):
            for f in range(self.n_f):
                g = (f % self.chips_per_row) * CORES + d % CORES
                t = (g + shift) % self.members
                td = d // CORES * CORES + t % CORES
                tf = f // self.chips_per_row * self.chips_per_row + t // CORES
                pairs.append((d * self.n_f + f, td * self.n_f + tf))
        return pairs

    def to_member(self, x, shift):
        return lax.ppermute(x, ("dp", "fsdp"), self.shift_pairs(shift))


class Schedule:
    def __init__(self, plan):
        self.plan = plan
        self.makers, self.running, self.waiting, self.result = {}, {}, {}, {}

    def add(self, name, maker, operands):
        self.makers[name] = (maker, operands)

    def step(self, name, value):
        try:
            chain = self.running[name]
            self.waiting[name] = next(chain) if value is None else chain.send(value)
        except StopIteration as end:
            self.waiting.pop(name, None)
            self.result[name] = end.value

    def start(self, name, operands):
        self.running[name] = self.makers[name][0](*operands)
        self.step(name, None)

    def tick(self, point, value):
        names = [n for n in self.plan.get(point, ()) if n not in self.result]
        arrived = {n: self.waiting[n] for n in names if n in self.running}
        fresh = [n for n in names if n not in self.running]
        ready = {n: self.makers[n][1]() for n in fresh if n not in LATE}
        value, arrived, ready = lax.optimization_barrier((value, arrived, ready))
        for name in arrived:
            self.step(name, arrived[name])
        for name in fresh:
            self.start(name, ready[name] if name in ready else self.makers[name][1]())
        return value

    def get(self, name):
        return self.finish(name)[0]

    def finish(self, *names):
        while any(n not in self.result for n in names):
            for name in names:
                if name not in self.running:
                    self.start(name, self.makers[name][1]())
                elif name not in self.result:
                    self.step(name, self.waiting[name])
        return [self.result[n] for n in names]


def dot_nt(a, b):
    return lax.dot_general(a, b, (((1,), (1,)), ((), ())), preferred_element_type=F32)


def dot_nn(a, b):
    return lax.dot_general(a, b, (((1,), (0,)), ((), ())), preferred_element_type=F32)


def dot_tn(a, b):
    return lax.dot_general(a, b, (((0,), (0,)), ((), ())), preferred_element_type=F32)


def head_only(x, head):
    lane = lax.broadcasted_iota(jnp.int32, x.shape, 1)
    keep = (lane >= HEAD_DIM) if head else (lane < HEAD_DIM)
    return jnp.where(keep, x, jnp.zeros_like(x))


def attend_kernel(chunks, q_step, *refs):
    q_ref = refs[0]
    k_refs = refs[1 : 1 + chunks]
    v_refs = refs[1 + chunks : 1 + 2 * chunks]
    seg_q_ref, seg_k_ref = refs[1 + 2 * chunks : 3 + 2 * chunks]
    o_ref, lse_ref = refs[-2:]
    tokens = q_ref.shape[0]
    for q0 in range(0, tokens, q_step):
        q = q_ref[q0 : q0 + q_step, :]
        seg_q = seg_q_ref[:, q0 : q0 + q_step]
        halves = []
        for head in range(2):
            q_head = head_only(q, head) * SCALING
            scores = []
            for c in range(chunks):
                s = dot_nt(k_refs[c][...], q_head)
                seg_k = seg_k_ref[c * tokens : (c + 1) * tokens, :]
                scores.append(jnp.where(seg_k == seg_q, s, NEGATIVE))
            highest = functools.reduce(
                jnp.maximum, [jnp.max(s, axis=0, keepdims=True) for s in scores]
            )
            powers = [jnp.exp(s - highest) for s in scores]
            norm = functools.reduce(
                jnp.add, [jnp.sum(p, axis=0, keepdims=True) for p in powers]
            )
            mixed = functools.reduce(
                jnp.add, [dot_tn(v_refs[c][...], powers[c].astype(BF)) for c in range(chunks)]
            )
            halves.append(mixed[head * HEAD_DIM : (head + 1) * HEAD_DIM, :] * (1.0 / norm))
            lse_ref[0, head : head + 1, q0 : q0 + q_step] = highest + jnp.log(norm)
        both = jnp.concatenate(halves, axis=0)
        o_ref[q0 : q0 + q_step, :] = both.T.astype(BF)


def attend_back_kernel(chunks, q_step, *refs):
    q_ref = refs[0]
    k_refs = refs[1 : 1 + chunks]
    v_refs = refs[1 + chunks : 1 + 2 * chunks]
    do_ref, lse_ref, seg_q_ref, seg_k_ref = refs[1 + 2 * chunks : 5 + 2 * chunks]
    dq_ref, own_ref, *other_refs = refs[-2 - chunks : -1]
    acc_ref = refs[-1]
    tokens = q_ref.shape[0]
    first = True
    for q0 in range(0, tokens, q_step):
        q = q_ref[q0 : q0 + q_step, :]
        do = do_ref[q0 : q0 + q_step, :]
        seg_q = seg_q_ref[:, q0 : q0 + q_step]
        halves = []
        for head in range(2):
            q_head = head_only(q, head) * SCALING
            do_head = head_only(do, head)
            lse = lse_ref[0, head : head + 1, q0 : q0 + q_step]
            probs, d_probs = [], []
            for c in range(chunks):
                s = dot_nt(k_refs[c][...], q_head)
                seg_k = seg_k_ref[c * tokens : (c + 1) * tokens, :]
                s = jnp.where(seg_k == seg_q, s, NEGATIVE)
                probs.append(jnp.exp(s - lse))
                d_probs.append(dot_nt(v_refs[c][...], do_head))
            offset = functools.reduce(
                jnp.add,
                [jnp.sum(p * d, axis=0, keepdims=True) for p, d in zip(probs, d_probs)],
            )
            dq_t = None
            for c in range(chunks):
                ds = (probs[c] * (d_probs[c] - offset)).astype(BF)
                dk = dot_nn(ds, q_head)
                dv = dot_nn(probs[c].astype(BF), do_head)
                term = dot_tn(k_refs[c][...], ds)
                dq_t = term if dq_t is None else dq_t + term
                if first:
                    acc_ref[c, 0] = dk
                    acc_ref[c, 1] = dv
                else:
                    acc_ref[c, 0] += dk
                    acc_ref[c, 1] += dv
            first = False
            halves.append(dq_t[head * HEAD_DIM : (head + 1) * HEAD_DIM, :])
        both = jnp.concatenate(halves, axis=0) * SCALING
        dq_ref[q0 : q0 + q_step, :] = both.T.astype(BF)
    own_ref[...] = acc_ref[0]
    for c in range(1, chunks):
        other_refs[c - 1][...] = acc_ref[c].astype(BF)


def attention_specs(qkv, others, first):
    block = (qkv.shape[0], PAIR)
    pairs = HEADS // 2
    at = lambda offset: pl.BlockSpec(block, lambda i: (0, offset + first + i))
    operands = [qkv, qkv] + others + [qkv] + others
    specs = [at(0), at(pairs)] + [at(0) for _ in others] + [at(2 * pairs)] + [at(pairs) for _ in others]
    return operands, specs


def whole(shape):
    return pl.BlockSpec(shape, lambda i: (0,) * len(shape))


def attend(qkv, others, seg_q, seg_k, first, count, done=None):
    operands, specs = attention_specs(qkv, others, first)
    tokens, length = qkv.shape[0], seg_k.shape[0]
    operands += [seg_q, seg_k]
    specs += [whole((1, tokens)), whole((length, 1))]
    aliases = {}
    if done is not None:
        aliases = {len(operands): 0, len(operands) + 1: 1}
        operands += list(done)
        specs += [pl.BlockSpec(memory_space=pl.ANY)] * 2
    return pl.pallas_call(
        functools.partial(attend_kernel, 1 + len(others), min(256, tokens)),
        grid=(count,),
        in_specs=specs,
        out_specs=[
            pl.BlockSpec((tokens, PAIR), lambda i: (0, first + i)),
            pl.BlockSpec((1, 2, tokens), lambda i: (first + i, 0, 0)),
        ],
        out_shape=[
            jax.ShapeDtypeStruct((tokens, HEADS * HEAD_DIM), BF),
            jax.ShapeDtypeStruct((HEADS // 2, 2, tokens), F32),
        ],
        input_output_aliases=aliases,
        compiler_params=pltpu.CompilerParams(vmem_limit_bytes=40 * 2**20),
        cost_estimate=pl.CostEstimate(
            flops=16 * tokens * length * count * PAIR,
            bytes_accessed=8 * length * count * PAIR,
            transcendentals=2 * tokens * length * count,
        ),
        name="attend",
    )(*operands)


def attend_back(qkv, others, d_mixture, lse, seg_q, seg_k, first, count, done=None):
    operands, specs = attention_specs(qkv, others, first)
    chunks = 1 + len(others)
    tokens, length = qkv.shape[0], seg_k.shape[0]
    width = HEADS * HEAD_DIM
    flat = pl.BlockSpec((tokens, PAIR), lambda i: (0, first + i))
    stacked = pl.BlockSpec((2, tokens, PAIR), lambda i: (0, 0, first + i))
    operands += [d_mixture, lse, seg_q, seg_k]
    specs += [
        flat,
        pl.BlockSpec((1, 2, tokens), lambda i: (first + i, 0, 0)),
        whole((1, tokens)),
        whole((length, 1)),
    ]
    aliases = {}
    if done is not None:
        aliases = {len(operands) + n: n for n in range(len(done))}
        operands += list(done)
        specs += [pl.BlockSpec(memory_space=pl.ANY)] * len(done)
    return pl.pallas_call(
        functools.partial(attend_back_kernel, chunks, min(256, tokens)),
        grid=(count,),
        in_specs=specs,
        out_specs=[flat, stacked] + [stacked for _ in others],
        out_shape=[
            jax.ShapeDtypeStruct((tokens, width), BF),
            jax.ShapeDtypeStruct((2, tokens, width), F32),
        ]
        + [jax.ShapeDtypeStruct((2, tokens, width), BF) for _ in others],
        scratch_shapes=[pltpu.VMEM((chunks, 2, tokens, PAIR), F32)],
        input_output_aliases=aliases,
        compiler_params=pltpu.CompilerParams(vmem_limit_bytes=40 * 2**20),
        cost_estimate=pl.CostEstimate(
            flops=40 * tokens * length * count * PAIR,
            bytes_accessed=20 * length * count * PAIR,
            transcendentals=2 * tokens * length * count,
        ),
        name="attend_back",
    )(*operands)


def split_small(small, sizes):
    vectors, at = [], 0
    for size in sizes:
        vectors.append(small[:, at : at + size].reshape(-1).astype(F32))
        at += size
    return vectors


def layer_forward(grid, phase, tick, inputs, weights, seg_q, seg_k, result=None):
    width = inputs.shape[1]
    x_low = inputs.astype(BF)
    qkv_w, attn_w, qv_b, attn_b, attn_g, attn_s, inner_b, outer_b, ffn_g, ffn_s = weights(True)
    bias = jnp.concatenate([qv_b[:width], jnp.zeros((width,), F32), qv_b[width:]])
    qkv = (matrix_product(x_low, qkv_w) + bias).astype(BF)
    qkv = tick((phase, AT_QKV), qkv)
    key_value = qkv[:, width:]
    others = [grid.to_member(key_value, shift) for shift in range(1, grid.members)]
    half = HEADS // 4
    done = attend(qkv, others, seg_q, seg_k, 0, half)
    done = tick((phase, AT_HALF), done)
    mixture, lse = attend(qkv, others, seg_q, seg_k, half, HEADS // 2 - half, done)
    mixture = tick((phase, AT_MIX), mixture)
    branch = matrix_product(mixture, attn_w) + attn_b
    normed, normed_one, inv_one = layer_norm(inputs.astype(F32) + branch, attn_g, attn_s)
    normed = tick((phase, AT_NORM), normed)
    normed = tick((phase, AT_FFN), normed)
    inner_w, outer_w = weights(False)
    normed_low = normed.astype(BF)
    inner = matrix_product(normed_low, inner_w) + inner_b
    active, slope = gelu_both(inner)
    active = tick((phase, AT_ACTIVE), active.astype(BF))
    outer = matrix_product(active, outer_w) + outer_b
    output, normed_two, inv_two = layer_norm(normed + outer, ffn_g, ffn_s)
    if result is not None:
        result.append(output)
    output = tick((phase, AT_OUT), output)
    saved = (x_low, qkv, others, lse, mixture, normed_one, inv_one, normed_low, slope, active, normed_two, inv_two)
    return output, saved


def layer_backward(grid, phase, tick, give, upstream, weights, saved, seg_q, seg_k, result=None):
    qkv_w, attn_w, qv_b, attn_b, attn_g, attn_s, inner_b, outer_b, ffn_g, ffn_s = weights(True)
    inner_w, outer_w = weights(False)
    (x_low, qkv, others, lse, mixture, normed_one, inv_one, normed_low, slope, active, normed_two, inv_two) = saved
    grad_ffn_g = jnp.sum(upstream * normed_two, axis=0)
    grad_ffn_s = jnp.sum(upstream, axis=0)
    d_second = norm_back(upstream, normed_two, inv_two, ffn_g)
    d_outer = d_second.astype(BF)
    grad_outer_b = column_sum(d_outer)
    grad_outer_w = left_t(active, d_outer).astype(BF)
    give(AT_D_OUTER, grad_outer_w)
    d_outer, grad_outer_w = lax.optimization_barrier((d_outer, grad_outer_w))
    d_outer = tick((phase, AT_D_OUTER), d_outer)
    d_inner = (right_t(d_outer, outer_w) * slope).astype(BF)
    grad_inner_b = column_sum(d_inner)
    grad_inner_w = left_t(normed_low, d_inner).astype(BF)
    give(AT_D_INNER, grad_inner_w)
    d_inner, grad_inner_w = lax.optimization_barrier((d_inner, grad_inner_w))
    d_inner = tick((phase, AT_D_INNER), d_inner)
    d_normed = right_t(d_inner, inner_w) + d_second
    grad_attn_g = jnp.sum(d_normed * normed_one, axis=0)
    grad_attn_s = jnp.sum(d_normed, axis=0)
    d_first = norm_back(d_normed, normed_one, inv_one, attn_g)
    d_branch = d_first.astype(BF)
    grad_attn_b = column_sum(d_branch)
    grad_attn_w = left_t(mixture, d_branch).astype(BF)
    d_mixture = right_t(d_branch, attn_w).astype(BF)
    d_mixture = tick((phase, AT_D_MIX), d_mixture)
    half = HEADS // 4
    done = attend_back(qkv, others, d_mixture, lse, seg_q, seg_k, 0, half)
    done = tick((phase, AT_D_HALF), done)
    d_queries, own, *for_others = attend_back(
        qkv, others, d_mixture, lse, seg_q, seg_k, half, HEADS // 2 - half, done
    )
    d_queries = tick((phase, AT_D_QUERY), d_queries)
    for shift in range(1, grid.members):
        own = own + grid.to_member(for_others[shift - 1], -shift).astype(F32)
    own = own.astype(BF)
    d_qkv = jnp.concatenate([d_queries, own[0], own[1]], axis=1)
    grad_qv_b = jnp.concatenate([column_sum(d_queries), column_sum(own[1])])
    grad_qkv_w = left_t(x_low, d_qkv).astype(BF)
    small = (grad_qv_b, grad_attn_b, grad_attn_g, grad_attn_s, grad_inner_b, grad_outer_b, grad_ffn_g, grad_ffn_s)
    give(AT_D_QKV, grad_qkv_w, grad_attn_w, small)
    d_qkv = tick((phase, AT_D_QKV), d_qkv)
    d_input = right_t(d_qkv, qkv_w) + d_first
    if result is not None:
        result.append(d_input)
    return tick((phase, AT_D_INPUT), d_input)


def contrastive(vectors, positives):
    count, width = vectors.shape
    similarity = jnp.dot(vectors, vectors.T, precision=FULL_PRECISION) / (width * SOFTMAX_HEAT)
    ids = jnp.arange(count, dtype=jnp.int32)
    similarity = jnp.where(ids[:, None] == ids[None, :], NEGATIVE, similarity)
    highest = jnp.max(similarity, axis=1, keepdims=True)
    totals = highest + jnp.log(jnp.sum(jnp.exp(similarity - highest), axis=1, keepdims=True))
    positive = positives[:, None] == ids[None, :]
    loss = jnp.sum(totals) - jnp.sum(jnp.where(positive, similarity, 0.0))
    slope = (jnp.exp(similarity - totals) - positive.astype(F32)) / (width * SOFTMAX_HEAT)
    return loss, jnp.dot(slope + slope.T, vectors, precision=FULL_PRECISION)


def body(
    hidden,
    skip_tokens,
    backbone_cotangent,
    head_cotangent,
    starts,
    positives,
    qkv_weight,
    qv_bias,
    attn_weight,
    attn_bias,
    attn_gain,
    attn_shift,
    inner_weight,
    inner_bias,
    outer_weight,
    outer_bias,
    ffn_gain,
    ffn_shift,
):
    rows_dev, local, width = hidden.shape
    grid = Grid(rows_dev)
    tokens = rows_dev * local
    length = tokens * grid.members

    starts_both = jnp.stack([starts, grid.swap(starts, grid.f_bits)])
    from_other = jnp.where(grid.row_in_group // rows_dev == grid.core, 0, 1)
    my_starts = lax.dynamic_index_in_dim(starts_both, from_other, 0, keepdims=False)
    my_starts = lax.dynamic_index_in_dim(
        my_starts, grid.row_in_group % rows_dev, 0, keepdims=False
    )
    place = jnp.arange(tokens, dtype=jnp.int32)
    q_pos = grid.member * tokens + place
    k_pos = jnp.concatenate(
        [
            (grid.member - shift) % grid.members * tokens + place
            for shift in range(grid.members)
        ]
    )
    segment = lambda pos: jnp.sum((my_starts[:, None] <= pos[None, :]).astype(jnp.int32), axis=0) - 1
    seg_q = segment(q_pos)[None, :]
    seg_k = segment(k_pos)[:, None]
    cls_hot = (my_starts[:, None] == q_pos[None, :]).astype(F32)
    is_cls = jnp.any(my_starts[:, None] == q_pos[None, :], axis=0)[:, None]

    devices = grid.n_dp * grid.n_f
    vectors = (qv_bias, attn_bias, attn_gain, attn_shift, inner_bias, outer_bias, ffn_gain, ffn_shift)
    sizes = [v.shape[1] for v in vectors]
    rows = qkv_weight.shape[1]
    small_own = jnp.concatenate(vectors, axis=1).reshape(rows, -1)
    small_cols = small_own.shape[1]
    padded = -(-small_cols // 128) * 128
    small_own = jnp.pad(small_own, ((0, 0), (0, padded - small_cols)))
    schedule = Schedule(PLAN)
    tick = schedule.tick

    def gather_qkv(*parts):
        out = jnp.concatenate(parts, axis=1)
        out = yield from grid.gather_z(out)
        return (yield from grid.gather_split(out))

    def gather_ffn(inner, outer):
        deep = outer.shape[0] // inner.shape[0]
        out = jnp.concatenate([inner, outer.reshape(inner.shape[0], -1)], axis=1)
        out = yield from grid.gather_z(out)
        inner, outer = out[:, : inner.shape[1]], out[:, inner.shape[1] :]
        return (yield from grid.gather_two(inner, outer.reshape(inner.shape[0] * deep, -1)))

    schedule.add(QKV_1, gather_qkv, lambda: (qkv_weight[0], attn_weight[0], small_own))
    schedule.add(QKV_2, gather_qkv, lambda: (qkv_weight[1], attn_weight[1]))
    schedule.add(FFN_1, gather_ffn, lambda: (inner_weight[0], outer_weight[0]))
    schedule.add(FFN_2, gather_ffn, lambda: (inner_weight[1], outer_weight[1]))
    schedule.add(HIDDEN, grid.to_rows, lambda: (hidden,))
    schedule.add(
        SKIP, grid.to_rows, lambda: (jnp.concatenate([skip_tokens, head_cotangent], axis=2),)
    )
    schedule.add(COTS, grid.to_rows, lambda: (backbone_cotangent,))

    small = []

    def weights_of(layer, qkv_name, ffn_name):
        def get(is_qkv):
            if not is_qkv:
                return schedule.get(ffn_name)
            if not small:
                every = schedule.get(QKV_1)[:, -padded:][:, :small_cols]
                small.append(every.reshape(devices, 2, -1))
            pack = schedule.get(qkv_name)
            cut = qkv_weight.shape[2]
            return (pack[:, :cut], pack[:, cut : cut + width], *split_small(small[0][:, layer], sizes))

        return get

    backbone, head = weights_of(0, QKV_1, FFN_1), weights_of(1, QKV_2, FFN_2)

    def scatter_qkv(*parts):
        out = jnp.concatenate(parts, axis=1)
        out = yield from grid.scatter_split(out)
        return (yield from grid.scatter_z(out))

    core_first = lambda turned: [grid.f_bits] + grid.upper(turned)

    def scatter_z(inner, outer):
        deep = outer.shape[0] // inner.shape[0]
        out = jnp.concatenate([inner, outer.reshape(inner.shape[0], -1)], axis=1)
        out = yield from grid.scatter_z(out)
        return out[:, : inner.shape[1]], out[:, inner.shape[1] :].reshape(out.shape[0] * deep, -1)

    kept_small = []

    def give_to(outer_name, inner_name, ffn_name, qkv_name, last):
        def pack(grad_qkv, grad_attn, vectors):
            if not last:
                return grad_qkv, grad_attn
            cut = [
                jnp.concatenate([v.reshape(devices, -1) for v in kept], axis=1)
                for kept in (vectors, kept_small[0])
            ]
            flat = jnp.stack(cut, axis=1).reshape(devices * rows, small_cols).astype(BF)
            return grad_qkv, grad_attn, jnp.pad(flat, ((0, 0), (0, padded - small_cols)))

        def give(which, *grads):
            if which == AT_D_OUTER:
                schedule.add(outer_name, lambda g: grid.scatter(g, core_first(False)), lambda: grads)
            elif which == AT_D_INNER:
                schedule.add(inner_name, lambda g: grid.scatter(g, core_first(True)), lambda: grads)
                both = lambda: [v.astype(BF) for v in schedule.finish(inner_name, outer_name)]
                schedule.add(ffn_name, scatter_z, both)
            else:
                kept_small.append(grads[2])
                schedule.add(qkv_name, scatter_qkv, lambda: pack(*grads))

        return give

    shared = n_bits(grid.chips_per_row)
    cls_bits = list(range(shared, grid.f_bits)) + grid.upper(True)

    def gather_cls(states):
        own = jnp.dot(cls_hot, states, precision=FULL_PRECISION)[None]
        for bit in [grid.f_bits] + list(range(shared)):
            got = yield grid.swap(own, bit)
            own = own + got
        return (yield from grid.gather(own, cls_bits))

    first_states = []
    schedule.add(CLS, gather_cls, lambda: (first_states[0],))

    mark = jnp.zeros((8, 128), F32) + my_starts[0].astype(F32)
    for n in range(START_TICKS):
        mark = tick((START, n), mark)
    x = schedule.get(HIDDEN)
    first, saved_one = layer_forward(grid, F0, tick, x, backbone, seg_q, seg_k, first_states)
    for n in range(BETWEEN_TICKS):
        first = tick((BETWEEN, n), first)
    skip_and_cot = schedule.get(SKIP)
    head_in = jnp.where(is_cls, first, skip_and_cot[:, :width].astype(F32))
    second, saved_two = layer_forward(grid, F1, tick, head_in, head, seg_q, seg_k)

    both_out = jnp.concatenate([first.astype(BF), second.astype(BF)], axis=1)
    schedule.add(OUTS, grid.from_rows, lambda: (both_out,))
    head_up = tick((TURN, 0), skip_and_cot[:, width:]).astype(F32)
    give = give_to(OUTER_G2, INNER_G2, FFN_G2, QKV_G2, False)
    d_head_in = layer_backward(grid, B1, tick, give, head_up, head, saved_two, seg_q, seg_k)
    skip_grad = jnp.where(is_cls, 0.0, d_head_in).astype(BF)
    schedule.add(SKIP_BACK, grid.from_rows, lambda: (skip_grad,))
    contrast_loss, d_cls_all = contrastive(schedule.get(CLS).reshape(-1, width), positives)
    my_row = grid.dp // CORES * (CORES * rows_dev) + grid.row_in_group
    d_cls = lax.dynamic_slice_in_dim(d_cls_all, my_row * SEGS, SEGS, 0)
    cot = schedule.get(COTS)
    upstream = (
        cot.astype(F32)
        + jnp.where(is_cls, d_head_in, 0.0)
        + lax.dot_general(cls_hot, d_cls, (((0,), (0,)), ((), ())), precision=FULL_PRECISION)
    )
    upstream = tick((UP, 0), upstream)
    give = give_to(OUTER_G1, INNER_G1, FFN_G1, QKV_G1, True)
    schedule.add(HIDDEN_BACK, grid.from_rows, lambda: (d_input[0].astype(BF),))
    d_input = []
    layer_backward(grid, B0, tick, give, upstream, backbone, saved_one, seg_q, seg_k, d_input)
    mark = jnp.zeros((8, 128), F32)
    for n in range(END_TICKS):
        mark = tick((END, n), mark)
    names = [HIDDEN_BACK, SKIP_BACK, OUTS, FFN_G1, FFN_G2, QKV_G1, QKV_G2]
    hidden_back, skip_back, outs, (inner_1, outer_1), (inner_2, outer_2), qkv_1, qkv_2 = schedule.finish(*names)

    cut = qkv_weight.shape[2]
    pair = lambda a, b: jnp.stack([a, b]).astype(F32)
    small_g = qkv_1[:, -padded:][:, :small_cols].reshape(2, -1).astype(F32)
    cuts, at = [], 0
    for size in sizes:
        cuts.append(small_g[:, at : at + size])
        at += size
    return (
        contrast_loss,
        outs[:, :, :width],
        outs[:, :, width:],
        hidden_back.astype(F32),
        skip_back.astype(F32),
        pair(qkv_1[:, :cut], qkv_2[:, :cut]),
        cuts[0],
        pair(qkv_1[:, cut : cut + width], qkv_2[:, cut : cut + width]),
        cuts[1],
        cuts[2],
        cuts[3],
        pair(inner_1, inner_2),
        cuts[4],
        pair(outer_1, outer_2),
        cuts[5],
        cuts[6],
        cuts[7],
    )


def solution(mesh):
    rows = P("dp", "fsdp", None)
    matrix = P(None, ("dp", "fsdp"), None)
    vector = P(None, ("dp", "fsdp"))
    params = (
        matrix,
        vector,
        matrix,
        vector,
        vector,
        vector,
        matrix,
        vector,
        matrix,
        vector,
        vector,
        vector,
    )
    return jax.shard_map(
        body,
        mesh=mesh,
        in_specs=(rows, rows, rows, rows, P("dp", None), P()) + params,
        out_specs=(P(), rows, rows, rows, rows) + params,
        check_vma=False,
    )
```

```python
import functools

import jax
import jax.numpy as jnp
from jax import lax
from jax.experimental import pallas as pl
from jax.experimental.pallas import tpu as pltpu
from jax.sharding import PartitionSpec as P

HEADS = 12
HEAD_DIM = 64
SEGS = 8
CORES = 2

EPS = 1e-12
SOFTMAX_HEAT = 0.02
NEGATIVE = -1e30
FULL_PRECISION = lax.Precision.HIGHEST
SCALING = HEAD_DIM ** (-0.5)
PAIR = 2 * HEAD_DIM
BF = jnp.bfloat16
F32 = jnp.float32

(
    QKV_1, FFN_1, QKV_2, FFN_2, HIDDEN, SKIP, COTS, CLS, OUTS, HIDDEN_BACK,
    OUTER_G1, INNER_G1, FFN_G1, QKV_G1, OUTER_G2, INNER_G2, FFN_G2, QKV_G2,
) = range(18)
START, F0, BETWEEN, F1, TURN, B1, UP, B0, END = range(9)
AT_QKV, AT_HALF, AT_MIX, AT_NORM, AT_FFN, AT_ACTIVE, AT_OUT = range(7)
AT_D_OUTER, AT_D_INNER, AT_D_NORM, AT_D_MIX, AT_D_HALF, AT_D_QUERY, AT_D_QKV, AT_D_INPUT = range(8)
START_TICKS, BETWEEN_TICKS, END_TICKS = 7, 1, 4
LATE = (FFN_G1, FFN_G2)
PLAN = {
    (START, 0): [QKV_1],
    (START, 1): [QKV_1, FFN_1],
    (START, 2): [QKV_1, FFN_1],
    (START, 3): [QKV_1, FFN_1],
    (START, 4): [QKV_1, HIDDEN],
    (START, 5): [QKV_1, FFN_1],
    (START, 6): [QKV_1, HIDDEN, QKV_2],
    (F0, AT_QKV): [FFN_1, QKV_2, FFN_2],
    (F0, AT_HALF): [QKV_2, FFN_2],
    (F0, AT_MIX): [FFN_1, QKV_2, FFN_2],
    (F0, AT_NORM): [FFN_1, QKV_2, SKIP],
    (F0, AT_OUT): [QKV_2, FFN_2, CLS],
    (BETWEEN, 0): [QKV_2, SKIP, CLS],
    (F1, AT_QKV): [FFN_2, CLS],
    (F1, AT_HALF): [CLS],
    (F1, AT_MIX): [FFN_2, CLS],
    (F1, AT_NORM): [FFN_2, CLS],
    (B1, AT_D_OUTER): [OUTER_G2],
    (B1, AT_D_INNER): [OUTER_G2, INNER_G2],
    (B1, AT_D_MIX): [INNER_G2],
    (B1, AT_D_HALF): [COTS],
    (B1, AT_D_QUERY): [OUTER_G2, INNER_G2],
    (B1, AT_D_QKV): [OUTER_G2, INNER_G2, FFN_G2, QKV_G2, COTS],
    (UP, 0): [QKV_G2, OUTS],
    (B0, AT_D_OUTER): [OUTER_G1, FFN_G2],
    (B0, AT_D_INNER): [QKV_G2, OUTER_G1, INNER_G1],
    (B0, AT_D_MIX): [FFN_G2, INNER_G1],
    (B0, AT_D_HALF): [QKV_G2],
    (B0, AT_D_QUERY): [OUTER_G1, INNER_G1, QKV_G2, FFN_G2],
    (B0, AT_D_QKV): [OUTS, OUTER_G1, INNER_G1, QKV_G1, FFN_G1, QKV_G2],
    (B0, AT_D_INPUT): [QKV_G1, HIDDEN_BACK, QKV_G2],
    (END, 0): [QKV_G1, FFN_G1],
    (END, 1): [QKV_G1],
    (END, 2): [QKV_G1, FFN_G1, HIDDEN_BACK],
    (END, 3): [QKV_G1, FFN_G1],
}


def layer_norm(residual, norm_gain, norm_shift):
    average = jnp.mean(residual, axis=-1, keepdims=True)
    centred = residual - average
    inv_std = lax.rsqrt(jnp.mean(centred * centred, axis=-1, keepdims=True) + EPS)
    normed = centred * inv_std
    return (normed * norm_gain + norm_shift, normed, inv_std)


def norm_back(upstream, normed, inv_std, norm_gain):
    scaled = upstream * norm_gain
    return inv_std * (
        scaled
        - jnp.mean(scaled, axis=-1, keepdims=True)
        - normed * jnp.mean(scaled * normed, axis=-1, keepdims=True)
    )


def gelu_both(v):
    phi_cdf = 0.5 * (1.0 + lax.erf(v * 0.7071067811865476))
    phi_pdf = jnp.exp(-0.5 * v * v) * 0.3989422804014327
    return v * phi_cdf, phi_cdf + v * phi_pdf


def matrix_product(first_op, second_op):
    return jnp.dot(first_op, second_op, preferred_element_type=F32)


def left_t(first_op, second_op):
    return lax.dot_general(
        first_op, second_op, (((0,), (0,)), ((), ())), preferred_element_type=F32
    )


def right_t(first_op, second_op):
    return lax.dot_general(
        first_op, second_op, (((1,), (1,)), ((), ())), preferred_element_type=F32
    )


def column_sum(inputs):
    return jnp.sum(inputs.astype(F32), axis=0)


def n_bits(count):
    return count.bit_length() - 1


class Grid:
    def __init__(self, rows_dev):
        self.n_dp = lax.axis_size("dp")
        self.n_f = lax.axis_size("fsdp")
        self.f_bits = n_bits(self.n_f)
        self.d_bits = n_bits(self.n_dp)
        self.dp = lax.axis_index("dp")
        self.f = lax.axis_index("fsdp")
        self.rows_dev = rows_dev
        self.chips_per_row = self.n_f // (CORES * rows_dev)
        self.members = CORES * self.chips_per_row
        self.core = self.dp % CORES
        self.row_in_group = self.f // self.chips_per_row
        self.member = (self.f % self.chips_per_row) * CORES + self.core

    def my_bit(self, bit):
        if bit < self.f_bits:
            return (self.f >> bit) & 1
        return (self.dp >> (bit - self.f_bits)) & 1

    def swap(self, x, bit):
        if bit < self.f_bits:
            return lax.ppermute(x, "fsdp", [(i, i ^ (1 << bit)) for i in range(self.n_f)])
        flip = 1 << (bit - self.f_bits)
        return lax.ppermute(x, "dp", [(i, i ^ flip) for i in range(self.n_dp)])

    def upper(self, turned):
        bits = list(range(self.f_bits + 1, self.f_bits + self.d_bits))
        return bits if turned else bits[::-1]

    def join(self, own, other, bit, have):
        place = sum(1 for b in have if b > bit)
        mine = self.my_bit(bit) == 0
        low = jnp.where(mine, own, other)
        high = jnp.where(mine, other, own)
        return lax.optimization_barrier(jnp.stack([low, high], axis=place))

    def gather(self, x, bits):
        out = x
        for n, bit in enumerate(bits):
            other = yield self.swap(out, bit)
            out = self.join(out, other, bit, bits[:n])
        return out.reshape((-1,) + x.shape[1:])

    def gather_z(self, x):
        if self.n_f != 4:
            return (yield from self.gather(x, list(range(self.f_bits))))
        other = yield self.swap(x, 0)
        pair = self.join(x, other, 0, [])
        middle = yield lax.ppermute(pair, "fsdp", [(1, 2), (2, 1)])
        outer = yield lax.ppermute(middle, "fsdp", [(1, 0), (2, 3)])
        inside = (self.f == 1) | (self.f == 2)
        out = self.join(pair, jnp.where(inside, middle, outer), 1, [0])
        return out.reshape((-1,) + x.shape[1:])

    def scatter_z(self, x):
        if self.n_f != 4:
            return (yield from self.scatter(x, list(range(self.f_bits))[::-1]))
        out = x.reshape((2, 2, -1) + x.shape[1:])
        kept, sent = self.halves(out, 1, [1, 0])
        inward = yield lax.ppermute(sent, "fsdp", [(0, 1), (3, 2)])
        summed = (sent.astype(F32) + inward.astype(F32)).astype(BF)
        middle = yield lax.ppermute(summed, "fsdp", [(1, 2), (2, 1)])
        out = (kept.astype(F32) + middle.astype(F32)).astype(BF)
        kept, sent = self.halves(out, 0, [0])
        got = yield self.swap(sent, 0)
        return (kept.astype(F32) + got.astype(F32)).astype(BF)

    def gather_two(self, x, y):
        outs = [x, y]
        ways = [self.upper(False), self.upper(True)]
        for n in range(self.d_bits - 1):
            others = yield [self.swap(o, way[n]) for o, way in zip(outs, ways)]
            outs = [
                self.join(o, other, way[n], way[:n])
                for o, other, way in zip(outs, others, ways)
            ]
        core = self.f_bits
        others = yield [self.swap(o, core) for o in outs]
        outs = [self.join(o, other, core, ways[0]) for o, other in zip(outs, others)]
        return [o.reshape((-1,) + v.shape[1:]) for o, v in zip(outs, (x, y))]

    def gather_split(self, x):
        half = x.shape[0] // 2
        outs = [x[:half], x[half:]]
        ways = [self.upper(False), self.upper(True)]
        for n in range(self.d_bits - 1):
            others = yield [self.swap(o, way[n]) for o, way in zip(outs, ways)]
            outs = [
                self.join(o, other, way[n], way[:n])
                for o, other, way in zip(outs, others, ways)
            ]
        out = jnp.concatenate(outs, axis=self.d_bits - 1)
        core = self.f_bits
        other = yield self.swap(out, core)
        return self.join(out, other, core, ways[0]).reshape((-1,) + x.shape[1:])

    def halves(self, x, bit, left):
        place = left.index(bit)
        mine = self.my_bit(bit)
        pick = lambda at: lax.dynamic_index_in_dim(x, at, place, keepdims=False)
        return pick(mine), pick(1 - mine)

    def scatter(self, x, bits):
        left = sorted(bits, reverse=True)
        out = x.reshape((2,) * len(bits) + (-1,) + x.shape[1:])
        for bit in bits:
            kept, sent = self.halves(out, bit, left)
            got = yield self.swap(sent, bit)
            left.remove(bit)
            out = (kept.astype(F32) + got.astype(F32)).astype(BF)
        return out

    def scatter_split(self, x):
        left = list(range(self.f_bits + self.d_bits - 1, self.f_bits - 1, -1))
        out = x.reshape((2,) * self.d_bits + (2, -1) + x.shape[1:])
        kept, sent = self.halves(out, self.f_bits, left)
        got = yield self.swap(sent, self.f_bits)
        out = (kept.astype(F32) + got.astype(F32)).astype(BF)
        left.remove(self.f_bits)
        outs = [lax.index_in_dim(out, h, len(left), keepdims=False) for h in range(2)]
        ways = [self.upper(True), self.upper(False)]
        lefts = [list(left), list(left)]
        for n in range(self.d_bits - 1):
            pairs = [self.halves(o, way[n], l) for o, way, l in zip(outs, ways, lefts)]
            gots = yield [self.swap(sent, way[n]) for (_, sent), way in zip(pairs, ways)]
            outs = [
                (kept.astype(F32) + got.astype(F32)).astype(BF)
                for (kept, _), got in zip(pairs, gots)
            ]
            for l, way in zip(lefts, ways):
                l.remove(way[n])
        return jnp.concatenate(outs, axis=0)

    def source(self, k):
        pairs = []
        for d in range(self.n_dp):
            for f in range(self.n_f):
                base, c = d // CORES * CORES, d % CORES
                b = (f + k) % self.rows_dev
                g = f // self.rows_dev
                row = self.rows_dev * c + b
                target_f = row * self.chips_per_row + g // CORES
                target_d = base + g % CORES
                pairs.append((d * self.n_f + f, target_d * self.n_f + target_f))
        return pairs

    def to_rows(self, x):
        got = []
        for k in range(self.rows_dev):
            block = lax.dynamic_index_in_dim(x, (self.f + k) % self.rows_dev, 0, keepdims=False)
            got.append(lax.ppermute(block, ("dp", "fsdp"), self.source(k)))
        got = yield got
        got = jnp.stack(got)
        b = self.row_in_group % self.rows_dev
        return jnp.concatenate(
            [
                lax.dynamic_index_in_dim(got, (b - p) % self.rows_dev, 0, keepdims=False)
                for p in range(self.rows_dev)
            ]
        )

    def from_rows(self, y):
        parts = y.reshape((self.rows_dev, -1) + y.shape[1:])
        b = self.row_in_group % self.rows_dev
        got = []
        for k in range(self.rows_dev):
            block = lax.dynamic_index_in_dim(parts, (b - k) % self.rows_dev, 0, keepdims=False)
            back = [(t, s) for s, t in self.source(k)]
            got.append(lax.ppermute(block, ("dp", "fsdp"), back))
        got = yield got
        got = jnp.stack(got)
        return jnp.stack(
            [
                lax.dynamic_index_in_dim(got, (row - self.f) % self.rows_dev, 0, keepdims=False)
                for row in range(self.rows_dev)
            ]
        )

    def shift_pairs(self, shift):
        pairs = []
        for d in range(self.n_dp):
            for f in range(self.n_f):
                g = (f % self.chips_per_row) * CORES + d % CORES
                t = (g + shift) % self.members
                td = d // CORES * CORES + t % CORES
                tf = f // self.chips_per_row * self.chips_per_row + t // CORES
                pairs.append((d * self.n_f + f, td * self.n_f + tf))
        return pairs

    def to_member(self, x, shift):
        return lax.ppermute(x, ("dp", "fsdp"), self.shift_pairs(shift))


class Schedule:
    def __init__(self, plan):
        self.plan = plan
        self.makers, self.running, self.waiting, self.result = {}, {}, {}, {}

    def add(self, name, maker, operands):
        self.makers[name] = (maker, operands)

    def step(self, name, value):
        try:
            chain = self.running[name]
            self.waiting[name] = next(chain) if value is None else chain.send(value)
        except StopIteration as end:
            self.waiting.pop(name, None)
            self.result[name] = end.value

    def start(self, name, operands):
        self.running[name] = self.makers[name][0](*operands)
        self.step(name, None)

    def tick(self, point, value):
        names = [n for n in self.plan.get(point, ()) if n not in self.result]
        arrived = {n: self.waiting[n] for n in names if n in self.running}
        fresh = [n for n in names if n not in self.running]
        ready = {n: self.makers[n][1]() for n in fresh if n not in LATE}
        value, arrived, ready = lax.optimization_barrier((value, arrived, ready))
        for name in arrived:
            self.step(name, arrived[name])
        for name in fresh:
            self.start(name, ready[name] if name in ready else self.makers[name][1]())
        return value

    def get(self, name):
        return self.finish(name)[0]

    def finish(self, *names):
        while any(n not in self.result for n in names):
            for name in names:
                if name not in self.running:
                    self.start(name, self.makers[name][1]())
                elif name not in self.result:
                    self.step(name, self.waiting[name])
        return [self.result[n] for n in names]


def dot_nt(a, b):
    return lax.dot_general(a, b, (((1,), (1,)), ((), ())), preferred_element_type=F32)


def dot_nn(a, b):
    return lax.dot_general(a, b, (((1,), (0,)), ((), ())), preferred_element_type=F32)


def dot_tn(a, b):
    return lax.dot_general(a, b, (((0,), (0,)), ((), ())), preferred_element_type=F32)


def head_only(x, head):
    lane = lax.broadcasted_iota(jnp.int32, x.shape, 1)
    keep = (lane >= HEAD_DIM) if head else (lane < HEAD_DIM)
    return jnp.where(keep, x, jnp.zeros_like(x))


def attend_kernel(chunks, q_step, *refs):
    q_ref = refs[0]
    k_refs = refs[1 : 1 + chunks]
    v_refs = refs[1 + chunks : 1 + 2 * chunks]
    seg_q_ref, seg_k_ref = refs[1 + 2 * chunks : 3 + 2 * chunks]
    o_ref, lse_ref = refs[-2:]
    tokens = q_ref.shape[0]
    for q0 in range(0, tokens, q_step):
        q = q_ref[q0 : q0 + q_step, :]
        seg_q = seg_q_ref[:, q0 : q0 + q_step]
        halves = []
        for head in range(2):
            q_head = head_only(q, head) * SCALING
            scores = []
            for c in range(chunks):
                s = dot_nt(k_refs[c][...], q_head)
                seg_k = seg_k_ref[c * tokens : (c + 1) * tokens, :]
                scores.append(jnp.where(seg_k == seg_q, s, NEGATIVE))
            highest = functools.reduce(
                jnp.maximum, [jnp.max(s, axis=0, keepdims=True) for s in scores]
            )
            powers = [jnp.exp(s - highest) for s in scores]
            norm = functools.reduce(
                jnp.add, [jnp.sum(p, axis=0, keepdims=True) for p in powers]
            )
            mixed = functools.reduce(
                jnp.add, [dot_tn(v_refs[c][...], powers[c].astype(BF)) for c in range(chunks)]
            )
            halves.append(mixed[head * HEAD_DIM : (head + 1) * HEAD_DIM, :] * (1.0 / norm))
            lse_ref[0, head : head + 1, q0 : q0 + q_step] = highest + jnp.log(norm)
        both = jnp.concatenate(halves, axis=0)
        o_ref[q0 : q0 + q_step, :] = both.T.astype(BF)


def attend_back_kernel(chunks, q_step, *refs):
    q_ref = refs[0]
    k_refs = refs[1 : 1 + chunks]
    v_refs = refs[1 + chunks : 1 + 2 * chunks]
    do_ref, lse_ref, seg_q_ref, seg_k_ref = refs[1 + 2 * chunks : 5 + 2 * chunks]
    dq_ref, own_ref, *other_refs = refs[-2 - chunks : -1]
    acc_ref = refs[-1]
    tokens = q_ref.shape[0]
    first = True
    for q0 in range(0, tokens, q_step):
        q = q_ref[q0 : q0 + q_step, :]
        do = do_ref[q0 : q0 + q_step, :]
        seg_q = seg_q_ref[:, q0 : q0 + q_step]
        halves = []
        for head in range(2):
            q_head = head_only(q, head) * SCALING
            do_head = head_only(do, head)
            lse = lse_ref[0, head : head + 1, q0 : q0 + q_step]
            probs, d_probs = [], []
            for c in range(chunks):
                s = dot_nt(k_refs[c][...], q_head)
                seg_k = seg_k_ref[c * tokens : (c + 1) * tokens, :]
                s = jnp.where(seg_k == seg_q, s, NEGATIVE)
                probs.append(jnp.exp(s - lse))
                d_probs.append(dot_nt(v_refs[c][...], do_head))
            offset = functools.reduce(
                jnp.add,
                [jnp.sum(p * d, axis=0, keepdims=True) for p, d in zip(probs, d_probs)],
            )
            dq_t = None
            for c in range(chunks):
                ds = (probs[c] * (d_probs[c] - offset)).astype(BF)
                dk = dot_nn(ds, q_head)
                dv = dot_nn(probs[c].astype(BF), do_head)
                term = dot_tn(k_refs[c][...], ds)
                dq_t = term if dq_t is None else dq_t + term
                if first:
                    acc_ref[c, 0] = dk
                    acc_ref[c, 1] = dv
                else:
                    acc_ref[c, 0] += dk
                    acc_ref[c, 1] += dv
            first = False
            halves.append(dq_t[head * HEAD_DIM : (head + 1) * HEAD_DIM, :])
        both = jnp.concatenate(halves, axis=0) * SCALING
        dq_ref[q0 : q0 + q_step, :] = both.T.astype(BF)
    own_ref[...] = acc_ref[0]
    for c in range(1, chunks):
        other_refs[c - 1][...] = acc_ref[c].astype(BF)


def attention_specs(qkv, others, first):
    block = (qkv.shape[0], PAIR)
    pairs = HEADS // 2
    at = lambda offset: pl.BlockSpec(block, lambda i: (0, offset + first + i))
    operands = [qkv, qkv] + others + [qkv] + others
    specs = [at(0), at(pairs)] + [at(0) for _ in others] + [at(2 * pairs)] + [at(pairs) for _ in others]
    return operands, specs


def whole(shape):
    return pl.BlockSpec(shape, lambda i: (0,) * len(shape))


def attend(qkv, others, seg_q, seg_k, first, count, done=None):
    operands, specs = attention_specs(qkv, others, first)
    tokens, length = qkv.shape[0], seg_k.shape[0]
    operands += [seg_q, seg_k]
    specs += [whole((1, tokens)), whole((length, 1))]
    aliases = {}
    if done is not None:
        aliases = {len(operands): 0, len(operands) + 1: 1}
        operands += list(done)
        specs += [pl.BlockSpec(memory_space=pl.ANY)] * 2
    return pl.pallas_call(
        functools.partial(attend_kernel, 1 + len(others), min(512, tokens)),
        grid=(count,),
        in_specs=specs,
        out_specs=[
            pl.BlockSpec((tokens, PAIR), lambda i: (0, first + i)),
            pl.BlockSpec((1, 2, tokens), lambda i: (first + i, 0, 0)),
        ],
        out_shape=[
            jax.ShapeDtypeStruct((tokens, HEADS * HEAD_DIM), BF),
            jax.ShapeDtypeStruct((HEADS // 2, 2, tokens), F32),
        ],
        input_output_aliases=aliases,
        compiler_params=pltpu.CompilerParams(vmem_limit_bytes=40 * 2**20),
        cost_estimate=pl.CostEstimate(
            flops=16 * tokens * length * count * PAIR,
            bytes_accessed=8 * length * count * PAIR,
            transcendentals=2 * tokens * length * count,
        ),
        name="attend",
    )(*operands)


def attend_back(qkv, others, d_mixture, lse, seg_q, seg_k, first, count, done=None):
    operands, specs = attention_specs(qkv, others, first)
    chunks = 1 + len(others)
    tokens, length = qkv.shape[0], seg_k.shape[0]
    width = HEADS * HEAD_DIM
    flat = pl.BlockSpec((tokens, PAIR), lambda i: (0, first + i))
    stacked = pl.BlockSpec((2, tokens, PAIR), lambda i: (0, 0, first + i))
    operands += [d_mixture, lse, seg_q, seg_k]
    specs += [
        flat,
        pl.BlockSpec((1, 2, tokens), lambda i: (first + i, 0, 0)),
        whole((1, tokens)),
        whole((length, 1)),
    ]
    aliases = {}
    if done is not None:
        aliases = {len(operands) + n: n for n in range(len(done))}
        operands += list(done)
        specs += [pl.BlockSpec(memory_space=pl.ANY)] * len(done)
    return pl.pallas_call(
        functools.partial(attend_back_kernel, chunks, min(512, tokens)),
        grid=(count,),
        in_specs=specs,
        out_specs=[flat, stacked] + [stacked for _ in others],
        out_shape=[
            jax.ShapeDtypeStruct((tokens, width), BF),
            jax.ShapeDtypeStruct((2, tokens, width), F32),
        ]
        + [jax.ShapeDtypeStruct((2, tokens, width), BF) for _ in others],
        scratch_shapes=[pltpu.VMEM((chunks, 2, tokens, PAIR), F32)],
        input_output_aliases=aliases,
        compiler_params=pltpu.CompilerParams(vmem_limit_bytes=40 * 2**20),
        cost_estimate=pl.CostEstimate(
            flops=40 * tokens * length * count * PAIR,
            bytes_accessed=20 * length * count * PAIR,
            transcendentals=2 * tokens * length * count,
        ),
        name="attend_back",
    )(*operands)


def split_small(small, sizes):
    vectors, at = [], 0
    for size in sizes:
        vectors.append(small[:, at : at + size].reshape(-1).astype(F32))
        at += size
    return vectors


def layer_forward(grid, phase, tick, inputs, weights, seg_q, seg_k, result=None):
    width = inputs.shape[1]
    x_low = inputs.astype(BF)
    qkv_w, attn_w, qv_b, attn_b, attn_g, attn_s, inner_b, outer_b, ffn_g, ffn_s = weights(True)
    bias = jnp.concatenate([qv_b[:width], jnp.zeros((width,), F32), qv_b[width:]])
    qkv = (matrix_product(x_low, qkv_w) + bias).astype(BF)
    qkv = tick((phase, AT_QKV), qkv)
    key_value = qkv[:, width:]
    others = [grid.to_member(key_value, shift) for shift in range(1, grid.members)]
    half = HEADS // 4
    done = attend(qkv, others, seg_q, seg_k, 0, half)
    done = tick((phase, AT_HALF), done)
    mixture, lse = attend(qkv, others, seg_q, seg_k, half, HEADS // 2 - half, done)
    mixture = tick((phase, AT_MIX), mixture)
    branch = matrix_product(mixture, attn_w) + attn_b
    normed, normed_one, inv_one = layer_norm(inputs.astype(F32) + branch, attn_g, attn_s)
    normed = tick((phase, AT_NORM), normed)
    normed = tick((phase, AT_FFN), normed)
    inner_w, outer_w = weights(False)
    normed_low = normed.astype(BF)
    inner = matrix_product(normed_low, inner_w) + inner_b
    active, slope = gelu_both(inner)
    active = tick((phase, AT_ACTIVE), active.astype(BF))
    outer = matrix_product(active, outer_w) + outer_b
    output, normed_two, inv_two = layer_norm(normed + outer, ffn_g, ffn_s)
    if result is not None:
        result.append(output)
    output = tick((phase, AT_OUT), output)
    saved = (x_low, qkv, others, lse, mixture, normed_one, inv_one, normed_low, slope, active, normed_two, inv_two)
    return output, saved


def layer_backward(grid, phase, tick, give, upstream, weights, saved, seg_q, seg_k, result=None):
    qkv_w, attn_w, qv_b, attn_b, attn_g, attn_s, inner_b, outer_b, ffn_g, ffn_s = weights(True)
    inner_w, outer_w = weights(False)
    (x_low, qkv, others, lse, mixture, normed_one, inv_one, normed_low, slope, active, normed_two, inv_two) = saved
    grad_ffn_g = jnp.sum(upstream * normed_two, axis=0)
    grad_ffn_s = jnp.sum(upstream, axis=0)
    d_second = norm_back(upstream, normed_two, inv_two, ffn_g)
    d_outer = d_second.astype(BF)
    grad_outer_b = column_sum(d_outer)
    grad_outer_w = left_t(active, d_outer).astype(BF)
    give(AT_D_OUTER, grad_outer_w)
    d_outer, grad_outer_w = lax.optimization_barrier((d_outer, grad_outer_w))
    d_outer = tick((phase, AT_D_OUTER), d_outer)
    d_inner = (right_t(d_outer, outer_w) * slope).astype(BF)
    grad_inner_b = column_sum(d_inner)
    grad_inner_w = left_t(normed_low, d_inner).astype(BF)
    give(AT_D_INNER, grad_inner_w)
    d_inner, grad_inner_w = lax.optimization_barrier((d_inner, grad_inner_w))
    d_inner = tick((phase, AT_D_INNER), d_inner)
    d_normed = right_t(d_inner, inner_w) + d_second
    grad_attn_g = jnp.sum(d_normed * normed_one, axis=0)
    grad_attn_s = jnp.sum(d_normed, axis=0)
    d_first = norm_back(d_normed, normed_one, inv_one, attn_g)
    d_branch = d_first.astype(BF)
    grad_attn_b = column_sum(d_branch)
    grad_attn_w = left_t(mixture, d_branch).astype(BF)
    d_mixture = right_t(d_branch, attn_w).astype(BF)
    d_mixture = tick((phase, AT_D_MIX), d_mixture)
    half = HEADS // 4
    done = attend_back(qkv, others, d_mixture, lse, seg_q, seg_k, 0, half)
    done = tick((phase, AT_D_HALF), done)
    d_queries, own, *for_others = attend_back(
        qkv, others, d_mixture, lse, seg_q, seg_k, half, HEADS // 2 - half, done
    )
    d_queries = tick((phase, AT_D_QUERY), d_queries)
    for shift in range(1, grid.members):
        own = own + grid.to_member(for_others[shift - 1], -shift).astype(F32)
    own = own.astype(BF)
    d_qkv = jnp.concatenate([d_queries, own[0], own[1]], axis=1)
    grad_qv_b = jnp.concatenate([column_sum(d_queries), column_sum(own[1])])
    grad_qkv_w = left_t(x_low, d_qkv).astype(BF)
    small = (grad_qv_b, grad_attn_b, grad_attn_g, grad_attn_s, grad_inner_b, grad_outer_b, grad_ffn_g, grad_ffn_s)
    give(AT_D_QKV, grad_qkv_w, grad_attn_w, small)
    d_qkv = tick((phase, AT_D_QKV), d_qkv)
    d_input = right_t(d_qkv, qkv_w) + d_first
    if result is not None:
        result.append(d_input)
    return tick((phase, AT_D_INPUT), d_input)


def contrastive(vectors, positives):
    count, width = vectors.shape
    similarity = jnp.dot(vectors, vectors.T, precision=FULL_PRECISION) / (width * SOFTMAX_HEAT)
    ids = jnp.arange(count, dtype=jnp.int32)
    similarity = jnp.where(ids[:, None] == ids[None, :], NEGATIVE, similarity)
    highest = jnp.max(similarity, axis=1, keepdims=True)
    totals = highest + jnp.log(jnp.sum(jnp.exp(similarity - highest), axis=1, keepdims=True))
    positive = positives[:, None] == ids[None, :]
    loss = jnp.sum(totals) - jnp.sum(jnp.where(positive, similarity, 0.0))
    slope = (jnp.exp(similarity - totals) - positive.astype(F32)) / (width * SOFTMAX_HEAT)
    return loss, jnp.dot(slope + slope.T, vectors, precision=FULL_PRECISION)


def body(
    hidden,
    skip_tokens,
    backbone_cotangent,
    head_cotangent,
    starts,
    positives,
    qkv_weight,
    qv_bias,
    attn_weight,
    attn_bias,
    attn_gain,
    attn_shift,
    inner_weight,
    inner_bias,
    outer_weight,
    outer_bias,
    ffn_gain,
    ffn_shift,
):
    rows_dev, local, width = hidden.shape
    grid = Grid(rows_dev)
    tokens = rows_dev * local
    length = tokens * grid.members

    starts_both = jnp.stack([starts, grid.swap(starts, grid.f_bits)])
    from_other = jnp.where(grid.row_in_group // rows_dev == grid.core, 0, 1)
    my_starts = lax.dynamic_index_in_dim(starts_both, from_other, 0, keepdims=False)
    my_starts = lax.dynamic_index_in_dim(
        my_starts, grid.row_in_group % rows_dev, 0, keepdims=False
    )
    place = jnp.arange(tokens, dtype=jnp.int32)
    q_pos = grid.member * tokens + place
    k_pos = jnp.concatenate(
        [
            (grid.member - shift) % grid.members * tokens + place
            for shift in range(grid.members)
        ]
    )
    segment = lambda pos: jnp.sum((my_starts[:, None] <= pos[None, :]).astype(jnp.int32), axis=0) - 1
    seg_q = segment(q_pos)[None, :]
    seg_k = segment(k_pos)[:, None]
    cls_hot = (my_starts[:, None] == q_pos[None, :]).astype(F32)
    is_cls = jnp.any(my_starts[:, None] == q_pos[None, :], axis=0)[:, None]

    devices = grid.n_dp * grid.n_f
    vectors = (qv_bias, attn_bias, attn_gain, attn_shift, inner_bias, outer_bias, ffn_gain, ffn_shift)
    sizes = [v.shape[1] for v in vectors]
    rows = qkv_weight.shape[1]
    small_own = jnp.concatenate(vectors, axis=1).reshape(rows, -1)
    small_cols = small_own.shape[1]
    padded = -(-small_cols // 128) * 128
    small_own = jnp.pad(small_own, ((0, 0), (0, padded - small_cols)))
    schedule = Schedule(PLAN)
    tick = schedule.tick

    def gather_qkv(*parts):
        out = jnp.concatenate(parts, axis=1)
        out = yield from grid.gather_z(out)
        return (yield from grid.gather_split(out))

    def gather_ffn(inner, outer):
        deep = outer.shape[0] // inner.shape[0]
        out = jnp.concatenate([inner, outer.reshape(inner.shape[0], -1)], axis=1)
        out = yield from grid.gather_z(out)
        inner, outer = out[:, : inner.shape[1]], out[:, inner.shape[1] :]
        return (yield from grid.gather_two(inner, outer.reshape(inner.shape[0] * deep, -1)))

    schedule.add(QKV_1, gather_qkv, lambda: (qkv_weight[0], attn_weight[0], small_own))
    schedule.add(QKV_2, gather_qkv, lambda: (qkv_weight[1], attn_weight[1]))
    schedule.add(FFN_1, gather_ffn, lambda: (inner_weight[0], outer_weight[0]))
    schedule.add(FFN_2, gather_ffn, lambda: (inner_weight[1], outer_weight[1]))
    schedule.add(HIDDEN, grid.to_rows, lambda: (hidden,))
    schedule.add(
        SKIP, grid.to_rows, lambda: (jnp.concatenate([skip_tokens, head_cotangent], axis=2),)
    )
    schedule.add(COTS, grid.to_rows, lambda: (backbone_cotangent,))

    small = []

    def weights_of(layer, qkv_name, ffn_name):
        def get(is_qkv):
            if not is_qkv:
                return schedule.get(ffn_name)
            if not small:
                every = schedule.get(QKV_1)[:, -padded:][:, :small_cols]
                small.append(every.reshape(devices, 2, -1))
            pack = schedule.get(qkv_name)
            cut = qkv_weight.shape[2]
            return (pack[:, :cut], pack[:, cut : cut + width], *split_small(small[0][:, layer], sizes))

        return get

    backbone, head = weights_of(0, QKV_1, FFN_1), weights_of(1, QKV_2, FFN_2)

    def scatter_qkv(*parts):
        out = jnp.concatenate(parts, axis=1)
        out = yield from grid.scatter_split(out)
        return (yield from grid.scatter_z(out))

    core_first = lambda turned: [grid.f_bits] + grid.upper(turned)

    def scatter_z(inner, outer):
        deep = outer.shape[0] // inner.shape[0]
        out = jnp.concatenate([inner, outer.reshape(inner.shape[0], -1)], axis=1)
        out = yield from grid.scatter_z(out)
        return out[:, : inner.shape[1]], out[:, inner.shape[1] :].reshape(out.shape[0] * deep, -1)

    kept_small = []

    def give_to(outer_name, inner_name, ffn_name, qkv_name, last):
        def pack(grad_qkv, grad_attn, vectors):
            if not last:
                return grad_qkv, grad_attn
            cut = [
                jnp.concatenate([v.reshape(devices, -1) for v in kept], axis=1)
                for kept in (vectors, kept_small[0])
            ]
            flat = jnp.stack(cut, axis=1).reshape(devices * rows, small_cols).astype(BF)
            return grad_qkv, grad_attn, jnp.pad(flat, ((0, 0), (0, padded - small_cols)))

        def give(which, *grads):
            if which == AT_D_OUTER:
                schedule.add(outer_name, lambda g: grid.scatter(g, core_first(False)), lambda: grads)
            elif which == AT_D_INNER:
                schedule.add(inner_name, lambda g: grid.scatter(g, core_first(True)), lambda: grads)
                both = lambda: [v.astype(BF) for v in schedule.finish(inner_name, outer_name)]
                schedule.add(ffn_name, scatter_z, both)
            else:
                kept_small.append(grads[2])
                schedule.add(qkv_name, scatter_qkv, lambda: pack(*grads))

        return give

    shared = n_bits(grid.chips_per_row)
    cls_bits = list(range(shared, grid.f_bits)) + grid.upper(True)

    def gather_cls(states):
        own = jnp.dot(cls_hot, states, precision=FULL_PRECISION)[None]
        for bit in [grid.f_bits] + list(range(shared)):
            got = yield grid.swap(own, bit)
            own = own + got
        return (yield from grid.gather(own, cls_bits))

    first_states = []
    schedule.add(CLS, gather_cls, lambda: (first_states[0],))

    mark = jnp.zeros((8, 128), F32) + my_starts[0].astype(F32)
    for n in range(START_TICKS):
        mark = tick((START, n), mark)
    x = schedule.get(HIDDEN)
    first, saved_one = layer_forward(grid, F0, tick, x, backbone, seg_q, seg_k, first_states)
    for n in range(BETWEEN_TICKS):
        first = tick((BETWEEN, n), first)
    skip_and_cot = schedule.get(SKIP)
    head_in = jnp.where(is_cls, first, skip_and_cot[:, :width].astype(F32))
    second, saved_two = layer_forward(grid, F1, tick, head_in, head, seg_q, seg_k)

    head_up = tick((TURN, 0), skip_and_cot[:, width:]).astype(F32)
    give = give_to(OUTER_G2, INNER_G2, FFN_G2, QKV_G2, False)
    d_head_in = layer_backward(grid, B1, tick, give, head_up, head, saved_two, seg_q, seg_k)
    skip_grad = jnp.where(is_cls, 0.0, d_head_in).astype(BF)
    results = jnp.concatenate([first.astype(BF), second.astype(BF), skip_grad], axis=1)
    schedule.add(OUTS, grid.from_rows, lambda: (results,))
    contrast_loss, d_cls_all = contrastive(schedule.get(CLS).reshape(-1, width), positives)
    my_row = grid.dp // CORES * (CORES * rows_dev) + grid.row_in_group
    d_cls = lax.dynamic_slice_in_dim(d_cls_all, my_row * SEGS, SEGS, 0)
    cot = schedule.get(COTS)
    upstream = (
        cot.astype(F32)
        + jnp.where(is_cls, d_head_in, 0.0)
        + lax.dot_general(cls_hot, d_cls, (((0,), (0,)), ((), ())), precision=FULL_PRECISION)
    )
    upstream = tick((UP, 0), upstream)
    give = give_to(OUTER_G1, INNER_G1, FFN_G1, QKV_G1, True)
    schedule.add(HIDDEN_BACK, grid.from_rows, lambda: (d_input[0].astype(BF),))
    d_input = []
    layer_backward(grid, B0, tick, give, upstream, backbone, saved_one, seg_q, seg_k, d_input)
    mark = jnp.zeros((8, 128), F32)
    for n in range(END_TICKS):
        mark = tick((END, n), mark)
    names = [HIDDEN_BACK, OUTS, FFN_G1, FFN_G2, QKV_G1, QKV_G2]
    hidden_back, outs, (inner_1, outer_1), (inner_2, outer_2), qkv_1, qkv_2 = schedule.finish(*names)

    cut = qkv_weight.shape[2]
    pair = lambda a, b: jnp.stack([a, b]).astype(F32)
    small_g = qkv_1[:, -padded:][:, :small_cols].reshape(2, -1).astype(F32)
    cuts, at = [], 0
    for size in sizes:
        cuts.append(small_g[:, at : at + size])
        at += size
    return (
        contrast_loss,
        outs[:, :, :width],
        outs[:, :, width : 2 * width],
        hidden_back.astype(F32),
        outs[:, :, 2 * width :].astype(F32),
        pair(qkv_1[:, :cut], qkv_2[:, :cut]),
        cuts[0],
        pair(qkv_1[:, cut : cut + width], qkv_2[:, cut : cut + width]),
        cuts[1],
        cuts[2],
        cuts[3],
        pair(inner_1, inner_2),
        cuts[4],
        pair(outer_1, outer_2),
        cuts[5],
        cuts[6],
        cuts[7],
    )


def solution(mesh):
    rows = P("dp", "fsdp", None)
    matrix = P(None, ("dp", "fsdp"), None)
    vector = P(None, ("dp", "fsdp"))
    params = (
        matrix,
        vector,
        matrix,
        vector,
        vector,
        vector,
        matrix,
        vector,
        matrix,
        vector,
        vector,
        vector,
    )
    return jax.shard_map(
        body,
        mesh=mesh,
        in_specs=(rows, rows, rows, rows, P("dp", None), P()) + params,
        out_specs=(P(), rows, rows, rows, rows) + params,
        check_vma=False,
    )
```

```python
import functools

import jax
import jax.numpy as jnp
from jax import lax
from jax.experimental import pallas as pl
from jax.experimental.pallas import tpu as pltpu
from jax.sharding import PartitionSpec as P

HEADS = 12
HEAD_DIM = 64
SEGS = 8
CORES = 2

EPS = 1e-12
SOFTMAX_HEAT = 0.02
NEGATIVE = -1e30
FULL_PRECISION = lax.Precision.HIGHEST
SCALING = HEAD_DIM ** (-0.5)
PAIR = 2 * HEAD_DIM
BF = jnp.bfloat16
F32 = jnp.float32

(
    QKV_1, FFN_1, QKV_2, FFN_2, HIDDEN, SKIP, COTS, CLS, OUTS, HIDDEN_BACK,
    OUTER_G1, INNER_G1, FFN_G1, QKV_G1, OUTER_G2, INNER_G2, FFN_G2, QKV_G2,
) = range(18)
START, F0, BETWEEN, F1, TURN, B1, UP, B0, END = range(9)
AT_QKV, AT_HALF, AT_MIX, AT_NORM, AT_FFN, AT_ACTIVE, AT_OUT = range(7)
AT_D_OUTER, AT_D_INNER, AT_D_NORM, AT_D_MIX, AT_D_HALF, AT_D_QUERY, AT_D_QKV, AT_D_INPUT = range(8)
START_TICKS, BETWEEN_TICKS, END_TICKS = 7, 1, 4
LATE = (FFN_G1, FFN_G2)
PLAN = {
    (START, 0): [QKV_1],
    (START, 1): [QKV_1, FFN_1],
    (START, 2): [QKV_1, FFN_1],
    (START, 3): [QKV_1, FFN_1],
    (START, 4): [QKV_1, HIDDEN],
    (START, 5): [QKV_1, FFN_1],
    (START, 6): [QKV_1, HIDDEN, QKV_2],
    (F0, AT_QKV): [FFN_1, QKV_2, FFN_2],
    (F0, AT_HALF): [QKV_2, FFN_2],
    (F0, AT_MIX): [FFN_1, QKV_2, FFN_2, SKIP],
    (F0, AT_NORM): [FFN_1, QKV_2],
    (F0, AT_OUT): [QKV_2, FFN_2, CLS],
    (BETWEEN, 0): [QKV_2, SKIP, CLS],
    (F1, AT_QKV): [FFN_2, CLS],
    (F1, AT_HALF): [CLS],
    (F1, AT_MIX): [FFN_2, CLS],
    (F1, AT_NORM): [FFN_2, CLS],
    (B1, AT_D_OUTER): [OUTER_G2],
    (B1, AT_D_INNER): [OUTER_G2, INNER_G2],
    (B1, AT_D_MIX): [INNER_G2],
    (B1, AT_D_HALF): [COTS],
    (B1, AT_D_QUERY): [OUTER_G2, INNER_G2],
    (B1, AT_D_QKV): [OUTER_G2, INNER_G2, FFN_G2, QKV_G2, COTS],
    (UP, 0): [QKV_G2, OUTS],
    (B0, AT_D_OUTER): [OUTER_G1, FFN_G2],
    (B0, AT_D_INNER): [QKV_G2, OUTER_G1, INNER_G1],
    (B0, AT_D_MIX): [FFN_G2, INNER_G1],
    (B0, AT_D_HALF): [QKV_G2],
    (B0, AT_D_QUERY): [OUTER_G1, INNER_G1, QKV_G2, FFN_G2],
    (B0, AT_D_QKV): [OUTS, OUTER_G1, INNER_G1, QKV_G1, FFN_G1, QKV_G2],
    (B0, AT_D_INPUT): [QKV_G1, HIDDEN_BACK, QKV_G2],
    (END, 0): [QKV_G1, FFN_G1],
    (END, 1): [QKV_G1],
    (END, 2): [QKV_G1, FFN_G1, HIDDEN_BACK],
    (END, 3): [QKV_G1, FFN_G1],
}


def layer_norm(residual, norm_gain, norm_shift):
    average = jnp.mean(residual, axis=-1, keepdims=True)
    centred = residual - average
    inv_std = lax.rsqrt(jnp.mean(centred * centred, axis=-1, keepdims=True) + EPS)
    normed = centred * inv_std
    return (normed * norm_gain + norm_shift, normed, inv_std)


def norm_back(upstream, normed, inv_std, norm_gain):
    scaled = upstream * norm_gain
    return inv_std * (
        scaled
        - jnp.mean(scaled, axis=-1, keepdims=True)
        - normed * jnp.mean(scaled * normed, axis=-1, keepdims=True)
    )


def gelu_both(v):
    phi_cdf = 0.5 * (1.0 + lax.erf(v * 0.7071067811865476))
    phi_pdf = jnp.exp(-0.5 * v * v) * 0.3989422804014327
    return v * phi_cdf, phi_cdf + v * phi_pdf


def matrix_product(first_op, second_op):
    return jnp.dot(first_op, second_op, preferred_element_type=F32)


def left_t(first_op, second_op):
    return lax.dot_general(
        first_op, second_op, (((0,), (0,)), ((), ())), preferred_element_type=F32
    )


def right_t(first_op, second_op):
    return lax.dot_general(
        first_op, second_op, (((1,), (1,)), ((), ())), preferred_element_type=F32
    )


def column_sum(inputs):
    return jnp.sum(inputs.astype(F32), axis=0)


def n_bits(count):
    return count.bit_length() - 1


class Grid:
    def __init__(self, rows_dev):
        self.n_dp = lax.axis_size("dp")
        self.n_f = lax.axis_size("fsdp")
        self.f_bits = n_bits(self.n_f)
        self.d_bits = n_bits(self.n_dp)
        self.dp = lax.axis_index("dp")
        self.f = lax.axis_index("fsdp")
        self.rows_dev = rows_dev
        self.chips_per_row = self.n_f // (CORES * rows_dev)
        self.members = CORES * self.chips_per_row
        self.core = self.dp % CORES
        self.row_in_group = self.f // self.chips_per_row
        self.member = (self.f % self.chips_per_row) * CORES + self.core

    def my_bit(self, bit):
        if bit < self.f_bits:
            return (self.f >> bit) & 1
        return (self.dp >> (bit - self.f_bits)) & 1

    def swap(self, x, bit):
        if bit < self.f_bits:
            return lax.ppermute(x, "fsdp", [(i, i ^ (1 << bit)) for i in range(self.n_f)])
        flip = 1 << (bit - self.f_bits)
        return lax.ppermute(x, "dp", [(i, i ^ flip) for i in range(self.n_dp)])

    def upper(self, turned):
        bits = list(range(self.f_bits + 1, self.f_bits + self.d_bits))
        return bits if turned else bits[::-1]

    def join(self, own, other, bit, have):
        place = sum(1 for b in have if b > bit)
        mine = self.my_bit(bit) == 0
        low = jnp.where(mine, own, other)
        high = jnp.where(mine, other, own)
        return lax.optimization_barrier(jnp.stack([low, high], axis=place))

    def gather(self, x, bits):
        out = x
        for n, bit in enumerate(bits):
            other = yield self.swap(out, bit)
            out = self.join(out, other, bit, bits[:n])
        return out.reshape((-1,) + x.shape[1:])

    def gather_z(self, x):
        if self.n_f != 4:
            return (yield from self.gather(x, list(range(self.f_bits))))
        other = yield self.swap(x, 0)
        pair = self.join(x, other, 0, [])
        middle = yield lax.ppermute(pair, "fsdp", [(1, 2), (2, 1)])
        outer = yield lax.ppermute(middle, "fsdp", [(1, 0), (2, 3)])
        inside = (self.f == 1) | (self.f == 2)
        out = self.join(pair, jnp.where(inside, middle, outer), 1, [0])
        return out.reshape((-1,) + x.shape[1:])

    def scatter_z(self, x):
        if self.n_f != 4:
            return (yield from self.scatter(x, list(range(self.f_bits))[::-1]))
        out = x.reshape((2, 2, -1) + x.shape[1:])
        kept, sent = self.halves(out, 1, [1, 0])
        inward = yield lax.ppermute(sent, "fsdp", [(0, 1), (3, 2)])
        summed = (sent.astype(F32) + inward.astype(F32)).astype(BF)
        middle = yield lax.ppermute(summed, "fsdp", [(1, 2), (2, 1)])
        out = (kept.astype(F32) + middle.astype(F32)).astype(BF)
        kept, sent = self.halves(out, 0, [0])
        got = yield self.swap(sent, 0)
        return (kept.astype(F32) + got.astype(F32)).astype(BF)

    def gather_two(self, x, y):
        outs = [x, y]
        ways = [self.upper(False), self.upper(True)]
        for n in range(self.d_bits - 1):
            others = yield [self.swap(o, way[n]) for o, way in zip(outs, ways)]
            outs = [
                self.join(o, other, way[n], way[:n])
                for o, other, way in zip(outs, others, ways)
            ]
        core = self.f_bits
        others = yield [self.swap(o, core) for o in outs]
        outs = [self.join(o, other, core, ways[0]) for o, other in zip(outs, others)]
        return [o.reshape((-1,) + v.shape[1:]) for o, v in zip(outs, (x, y))]

    def gather_split(self, x):
        half = x.shape[0] // 2
        outs = [x[:half], x[half:]]
        ways = [self.upper(False), self.upper(True)]
        for n in range(self.d_bits - 1):
            others = yield [self.swap(o, way[n]) for o, way in zip(outs, ways)]
            outs = [
                self.join(o, other, way[n], way[:n])
                for o, other, way in zip(outs, others, ways)
            ]
        out = jnp.concatenate(outs, axis=self.d_bits - 1)
        core = self.f_bits
        other = yield self.swap(out, core)
        return self.join(out, other, core, ways[0]).reshape((-1,) + x.shape[1:])

    def halves(self, x, bit, left):
        place = left.index(bit)
        mine = self.my_bit(bit)
        pick = lambda at: lax.dynamic_index_in_dim(x, at, place, keepdims=False)
        return pick(mine), pick(1 - mine)

    def scatter(self, x, bits):
        left = sorted(bits, reverse=True)
        out = x.reshape((2,) * len(bits) + (-1,) + x.shape[1:])
        for bit in bits:
            kept, sent = self.halves(out, bit, left)
            got = yield self.swap(sent, bit)
            left.remove(bit)
            out = (kept.astype(F32) + got.astype(F32)).astype(BF)
        return out

    def scatter_split(self, x):
        left = list(range(self.f_bits + self.d_bits - 1, self.f_bits - 1, -1))
        out = x.reshape((2,) * self.d_bits + (2, -1) + x.shape[1:])
        kept, sent = self.halves(out, self.f_bits, left)
        got = yield self.swap(sent, self.f_bits)
        out = (kept.astype(F32) + got.astype(F32)).astype(BF)
        left.remove(self.f_bits)
        outs = [lax.index_in_dim(out, h, len(left), keepdims=False) for h in range(2)]
        ways = [self.upper(True), self.upper(False)]
        lefts = [list(left), list(left)]
        for n in range(self.d_bits - 1):
            pairs = [self.halves(o, way[n], l) for o, way, l in zip(outs, ways, lefts)]
            gots = yield [self.swap(sent, way[n]) for (_, sent), way in zip(pairs, ways)]
            outs = [
                (kept.astype(F32) + got.astype(F32)).astype(BF)
                for (kept, _), got in zip(pairs, gots)
            ]
            for l, way in zip(lefts, ways):
                l.remove(way[n])
        return jnp.concatenate(outs, axis=0)

    def source(self, k):
        pairs = []
        for d in range(self.n_dp):
            for f in range(self.n_f):
                base, c = d // CORES * CORES, d % CORES
                b = (f + k) % self.rows_dev
                g = f // self.rows_dev
                row = self.rows_dev * c + b
                target_f = row * self.chips_per_row + g // CORES
                target_d = base + g % CORES
                pairs.append((d * self.n_f + f, target_d * self.n_f + target_f))
        return pairs

    def to_rows(self, x):
        got = []
        for k in range(self.rows_dev):
            block = lax.dynamic_index_in_dim(x, (self.f + k) % self.rows_dev, 0, keepdims=False)
            got.append(lax.ppermute(block, ("dp", "fsdp"), self.source(k)))
        got = yield got
        got = jnp.stack(got)
        b = self.row_in_group % self.rows_dev
        return jnp.concatenate(
            [
                lax.dynamic_index_in_dim(got, (b - p) % self.rows_dev, 0, keepdims=False)
                for p in range(self.rows_dev)
            ]
        )

    def from_rows(self, y):
        parts = y.reshape((self.rows_dev, -1) + y.shape[1:])
        b = self.row_in_group % self.rows_dev
        got = []
        for k in range(self.rows_dev):
            block = lax.dynamic_index_in_dim(parts, (b - k) % self.rows_dev, 0, keepdims=False)
            back = [(t, s) for s, t in self.source(k)]
            got.append(lax.ppermute(block, ("dp", "fsdp"), back))
        got = yield got
        got = jnp.stack(got)
        return jnp.stack(
            [
                lax.dynamic_index_in_dim(got, (row - self.f) % self.rows_dev, 0, keepdims=False)
                for row in range(self.rows_dev)
            ]
        )

    def shift_pairs(self, shift):
        pairs = []
        for d in range(self.n_dp):
            for f in range(self.n_f):
                g = (f % self.chips_per_row) * CORES + d % CORES
                t = (g + shift) % self.members
                td = d // CORES * CORES + t % CORES
                tf = f // self.chips_per_row * self.chips_per_row + t // CORES
                pairs.append((d * self.n_f + f, td * self.n_f + tf))
        return pairs

    def to_member(self, x, shift):
        return lax.ppermute(x, ("dp", "fsdp"), self.shift_pairs(shift))


class Schedule:
    def __init__(self, plan):
        self.plan = plan
        self.makers, self.running, self.waiting, self.result = {}, {}, {}, {}

    def add(self, name, maker, operands):
        self.makers[name] = (maker, operands)

    def step(self, name, value):
        try:
            chain = self.running[name]
            self.waiting[name] = next(chain) if value is None else chain.send(value)
        except StopIteration as end:
            self.waiting.pop(name, None)
            self.result[name] = end.value

    def start(self, name, operands):
        self.running[name] = self.makers[name][0](*operands)
        self.step(name, None)

    def tick(self, point, value):
        names = [n for n in self.plan.get(point, ()) if n not in self.result]
        arrived = {n: self.waiting[n] for n in names if n in self.running}
        fresh = [n for n in names if n not in self.running]
        ready = {n: self.makers[n][1]() for n in fresh if n not in LATE}
        value, arrived, ready = lax.optimization_barrier((value, arrived, ready))
        for name in arrived:
            self.step(name, arrived[name])
        for name in fresh:
            self.start(name, ready[name] if name in ready else self.makers[name][1]())
        return value

    def get(self, name):
        return self.finish(name)[0]

    def finish(self, *names):
        while any(n not in self.result for n in names):
            for name in names:
                if name not in self.running:
                    self.start(name, self.makers[name][1]())
                elif name not in self.result:
                    self.step(name, self.waiting[name])
        return [self.result[n] for n in names]


def dot_nt(a, b):
    return lax.dot_general(a, b, (((1,), (1,)), ((), ())), preferred_element_type=F32)


def dot_nn(a, b):
    return lax.dot_general(a, b, (((1,), (0,)), ((), ())), preferred_element_type=F32)


def dot_tn(a, b):
    return lax.dot_general(a, b, (((0,), (0,)), ((), ())), preferred_element_type=F32)


def head_only(x, head):
    lane = lax.broadcasted_iota(jnp.int32, x.shape, 1)
    keep = (lane >= HEAD_DIM) if head else (lane < HEAD_DIM)
    return jnp.where(keep, x, jnp.zeros_like(x))


def attend_kernel(chunks, q_step, *refs):
    q_ref = refs[0]
    k_refs = refs[1 : 1 + chunks]
    v_refs = refs[1 + chunks : 1 + 2 * chunks]
    seg_q_ref, seg_k_ref = refs[1 + 2 * chunks : 3 + 2 * chunks]
    o_ref, lse_ref = refs[-2:]
    tokens = q_ref.shape[0]
    for q0 in range(0, tokens, q_step):
        q = q_ref[q0 : q0 + q_step, :]
        seg_q = seg_q_ref[:, q0 : q0 + q_step]
        halves = []
        for head in range(2):
            q_head = head_only(q, head) * SCALING
            scores = []
            for c in range(chunks):
                s = dot_nt(k_refs[c][...], q_head)
                seg_k = seg_k_ref[c * tokens : (c + 1) * tokens, :]
                scores.append(jnp.where(seg_k == seg_q, s, NEGATIVE))
            highest = functools.reduce(
                jnp.maximum, [jnp.max(s, axis=0, keepdims=True) for s in scores]
            )
            powers = [jnp.exp(s - highest) for s in scores]
            norm = functools.reduce(
                jnp.add, [jnp.sum(p, axis=0, keepdims=True) for p in powers]
            )
            mixed = functools.reduce(
                jnp.add, [dot_tn(v_refs[c][...], powers[c].astype(BF)) for c in range(chunks)]
            )
            halves.append(mixed[head * HEAD_DIM : (head + 1) * HEAD_DIM, :] * (1.0 / norm))
            lse_ref[0, head : head + 1, q0 : q0 + q_step] = highest + jnp.log(norm)
        both = jnp.concatenate(halves, axis=0)
        o_ref[q0 : q0 + q_step, :] = both.T.astype(BF)


def attend_back_kernel(chunks, q_step, *refs):
    q_ref = refs[0]
    k_refs = refs[1 : 1 + chunks]
    v_refs = refs[1 + chunks : 1 + 2 * chunks]
    do_ref, lse_ref, seg_q_ref, seg_k_ref = refs[1 + 2 * chunks : 5 + 2 * chunks]
    dq_ref, own_ref, *other_refs = refs[-2 - chunks : -1]
    acc_ref = refs[-1]
    tokens = q_ref.shape[0]
    first = True
    for q0 in range(0, tokens, q_step):
        q = q_ref[q0 : q0 + q_step, :]
        do = do_ref[q0 : q0 + q_step, :]
        seg_q = seg_q_ref[:, q0 : q0 + q_step]
        halves = []
        for head in range(2):
            q_head = head_only(q, head) * SCALING
            do_head = head_only(do, head)
            lse = lse_ref[0, head : head + 1, q0 : q0 + q_step]
            probs, d_probs = [], []
            for c in range(chunks):
                s = dot_nt(k_refs[c][...], q_head)
                seg_k = seg_k_ref[c * tokens : (c + 1) * tokens, :]
                s = jnp.where(seg_k == seg_q, s, NEGATIVE)
                probs.append(jnp.exp(s - lse))
                d_probs.append(dot_nt(v_refs[c][...], do_head))
            offset = functools.reduce(
                jnp.add,
                [jnp.sum(p * d, axis=0, keepdims=True) for p, d in zip(probs, d_probs)],
            )
            dq_t = None
            for c in range(chunks):
                ds = (probs[c] * (d_probs[c] - offset)).astype(BF)
                dk = dot_nn(ds, q_head)
                dv = dot_nn(probs[c].astype(BF), do_head)
                term = dot_tn(k_refs[c][...], ds)
                dq_t = term if dq_t is None else dq_t + term
                if first:
                    acc_ref[c, 0] = dk
                    acc_ref[c, 1] = dv
                else:
                    acc_ref[c, 0] += dk
                    acc_ref[c, 1] += dv
            first = False
            halves.append(dq_t[head * HEAD_DIM : (head + 1) * HEAD_DIM, :])
        both = jnp.concatenate(halves, axis=0) * SCALING
        dq_ref[q0 : q0 + q_step, :] = both.T.astype(BF)
    own_ref[...] = acc_ref[0]
    for c in range(1, chunks):
        other_refs[c - 1][...] = acc_ref[c].astype(BF)


def attention_specs(qkv, others, first):
    block = (qkv.shape[0], PAIR)
    pairs = HEADS // 2
    at = lambda offset: pl.BlockSpec(block, lambda i: (0, offset + first + i))
    operands = [qkv, qkv] + others + [qkv] + others
    specs = [at(0), at(pairs)] + [at(0) for _ in others] + [at(2 * pairs)] + [at(pairs) for _ in others]
    return operands, specs


def whole(shape):
    return pl.BlockSpec(shape, lambda i: (0,) * len(shape))


def attend(qkv, others, seg_q, seg_k, first, count, done=None):
    operands, specs = attention_specs(qkv, others, first)
    tokens, length = qkv.shape[0], seg_k.shape[0]
    operands += [seg_q, seg_k]
    specs += [whole((1, tokens)), whole((length, 1))]
    aliases = {}
    if done is not None:
        aliases = {len(operands): 0, len(operands) + 1: 1}
        operands += list(done)
        specs += [pl.BlockSpec(memory_space=pl.ANY)] * 2
    return pl.pallas_call(
        functools.partial(attend_kernel, 1 + len(others), min(512, tokens)),
        grid=(count,),
        in_specs=specs,
        out_specs=[
            pl.BlockSpec((tokens, PAIR), lambda i: (0, first + i)),
            pl.BlockSpec((1, 2, tokens), lambda i: (first + i, 0, 0)),
        ],
        out_shape=[
            jax.ShapeDtypeStruct((tokens, HEADS * HEAD_DIM), BF),
            jax.ShapeDtypeStruct((HEADS // 2, 2, tokens), F32),
        ],
        input_output_aliases=aliases,
        compiler_params=pltpu.CompilerParams(vmem_limit_bytes=40 * 2**20),
        cost_estimate=pl.CostEstimate(
            flops=16 * tokens * length * count * PAIR,
            bytes_accessed=8 * length * count * PAIR,
            transcendentals=2 * tokens * length * count,
        ),
        name="attend",
    )(*operands)


def attend_back(qkv, others, d_mixture, lse, seg_q, seg_k, first, count, done=None):
    operands, specs = attention_specs(qkv, others, first)
    chunks = 1 + len(others)
    tokens, length = qkv.shape[0], seg_k.shape[0]
    width = HEADS * HEAD_DIM
    flat = pl.BlockSpec((tokens, PAIR), lambda i: (0, first + i))
    stacked = pl.BlockSpec((2, tokens, PAIR), lambda i: (0, 0, first + i))
    operands += [d_mixture, lse, seg_q, seg_k]
    specs += [
        flat,
        pl.BlockSpec((1, 2, tokens), lambda i: (first + i, 0, 0)),
        whole((1, tokens)),
        whole((length, 1)),
    ]
    aliases = {}
    if done is not None:
        aliases = {len(operands) + n: n for n in range(len(done))}
        operands += list(done)
        specs += [pl.BlockSpec(memory_space=pl.ANY)] * len(done)
    return pl.pallas_call(
        functools.partial(attend_back_kernel, chunks, min(512, tokens)),
        grid=(count,),
        in_specs=specs,
        out_specs=[flat, stacked] + [stacked for _ in others],
        out_shape=[
            jax.ShapeDtypeStruct((tokens, width), BF),
            jax.ShapeDtypeStruct((2, tokens, width), F32),
        ]
        + [jax.ShapeDtypeStruct((2, tokens, width), BF) for _ in others],
        scratch_shapes=[pltpu.VMEM((chunks, 2, tokens, PAIR), F32)],
        input_output_aliases=aliases,
        compiler_params=pltpu.CompilerParams(vmem_limit_bytes=40 * 2**20),
        cost_estimate=pl.CostEstimate(
            flops=40 * tokens * length * count * PAIR,
            bytes_accessed=20 * length * count * PAIR,
            transcendentals=2 * tokens * length * count,
        ),
        name="attend_back",
    )(*operands)


def split_small(small, sizes):
    vectors, at = [], 0
    for size in sizes:
        vectors.append(small[:, at : at + size].reshape(-1).astype(F32))
        at += size
    return vectors


def layer_forward(grid, phase, tick, inputs, weights, seg_q, seg_k, result=None):
    width = inputs.shape[1]
    x_low = inputs.astype(BF)
    qkv_w, attn_w, qv_b, attn_b, attn_g, attn_s, inner_b, outer_b, ffn_g, ffn_s = weights(True)
    bias = jnp.concatenate([qv_b[:width], jnp.zeros((width,), F32), qv_b[width:]])
    qkv = (matrix_product(x_low, qkv_w) + bias).astype(BF)
    qkv = tick((phase, AT_QKV), qkv)
    key_value = qkv[:, width:]
    others = [grid.to_member(key_value, shift) for shift in range(1, grid.members)]
    half = HEADS // 4
    done = attend(qkv, others, seg_q, seg_k, 0, half)
    done = tick((phase, AT_HALF), done)
    mixture, lse = attend(qkv, others, seg_q, seg_k, half, HEADS // 2 - half, done)
    mixture = tick((phase, AT_MIX), mixture)
    branch = matrix_product(mixture, attn_w) + attn_b
    normed, normed_one, inv_one = layer_norm(inputs.astype(F32) + branch, attn_g, attn_s)
    normed = tick((phase, AT_NORM), normed)
    normed = tick((phase, AT_FFN), normed)
    inner_w, outer_w = weights(False)
    normed_low = normed.astype(BF)
    inner = matrix_product(normed_low, inner_w) + inner_b
    active, slope = gelu_both(inner)
    active = tick((phase, AT_ACTIVE), active.astype(BF))
    outer = matrix_product(active, outer_w) + outer_b
    output, normed_two, inv_two = layer_norm(normed + outer, ffn_g, ffn_s)
    if result is not None:
        result.append(output)
    output = tick((phase, AT_OUT), output)
    saved = (x_low, qkv, others, lse, mixture, normed_one, inv_one, normed_low, slope, active, normed_two, inv_two)
    return output, saved


def layer_backward(grid, phase, tick, give, upstream, weights, saved, seg_q, seg_k, result=None):
    qkv_w, attn_w, qv_b, attn_b, attn_g, attn_s, inner_b, outer_b, ffn_g, ffn_s = weights(True)
    inner_w, outer_w = weights(False)
    (x_low, qkv, others, lse, mixture, normed_one, inv_one, normed_low, slope, active, normed_two, inv_two) = saved
    grad_ffn_g = jnp.sum(upstream * normed_two, axis=0)
    grad_ffn_s = jnp.sum(upstream, axis=0)
    d_second = norm_back(upstream, normed_two, inv_two, ffn_g)
    d_outer = d_second.astype(BF)
    grad_outer_b = column_sum(d_outer)
    grad_outer_w = left_t(active, d_outer).astype(BF)
    give(AT_D_OUTER, grad_outer_w)
    d_outer, grad_outer_w = lax.optimization_barrier((d_outer, grad_outer_w))
    d_outer = tick((phase, AT_D_OUTER), d_outer)
    d_inner = (right_t(d_outer, outer_w) * slope).astype(BF)
    grad_inner_b = column_sum(d_inner)
    grad_inner_w = left_t(normed_low, d_inner).astype(BF)
    give(AT_D_INNER, grad_inner_w)
    d_inner, grad_inner_w = lax.optimization_barrier((d_inner, grad_inner_w))
    d_inner = tick((phase, AT_D_INNER), d_inner)
    d_normed = right_t(d_inner, inner_w) + d_second
    grad_attn_g = jnp.sum(d_normed * normed_one, axis=0)
    grad_attn_s = jnp.sum(d_normed, axis=0)
    d_first = norm_back(d_normed, normed_one, inv_one, attn_g)
    d_branch = d_first.astype(BF)
    grad_attn_b = column_sum(d_branch)
    grad_attn_w = left_t(mixture, d_branch).astype(BF)
    d_mixture = right_t(d_branch, attn_w).astype(BF)
    d_mixture = tick((phase, AT_D_MIX), d_mixture)
    half = HEADS // 4
    done = attend_back(qkv, others, d_mixture, lse, seg_q, seg_k, 0, half)
    done = tick((phase, AT_D_HALF), done)
    d_queries, own, *for_others = attend_back(
        qkv, others, d_mixture, lse, seg_q, seg_k, half, HEADS // 2 - half, done
    )
    d_queries = tick((phase, AT_D_QUERY), d_queries)
    for shift in range(1, grid.members):
        own = own + grid.to_member(for_others[shift - 1], -shift).astype(F32)
    own = own.astype(BF)
    d_qkv = jnp.concatenate([d_queries, own[0], own[1]], axis=1)
    grad_qv_b = jnp.concatenate([column_sum(d_queries), column_sum(own[1])])
    grad_qkv_w = left_t(x_low, d_qkv).astype(BF)
    small = (grad_qv_b, grad_attn_b, grad_attn_g, grad_attn_s, grad_inner_b, grad_outer_b, grad_ffn_g, grad_ffn_s)
    give(AT_D_QKV, grad_qkv_w, grad_attn_w, small)
    d_qkv = tick((phase, AT_D_QKV), d_qkv)
    d_input = right_t(d_qkv, qkv_w) + d_first
    if result is not None:
        result.append(d_input)
    return tick((phase, AT_D_INPUT), d_input)


def contrastive(vectors, positives):
    count, width = vectors.shape
    similarity = jnp.dot(vectors, vectors.T, precision=FULL_PRECISION) / (width * SOFTMAX_HEAT)
    ids = jnp.arange(count, dtype=jnp.int32)
    similarity = jnp.where(ids[:, None] == ids[None, :], NEGATIVE, similarity)
    highest = jnp.max(similarity, axis=1, keepdims=True)
    totals = highest + jnp.log(jnp.sum(jnp.exp(similarity - highest), axis=1, keepdims=True))
    positive = positives[:, None] == ids[None, :]
    loss = jnp.sum(totals) - jnp.sum(jnp.where(positive, similarity, 0.0))
    slope = (jnp.exp(similarity - totals) - positive.astype(F32)) / (width * SOFTMAX_HEAT)
    return loss, jnp.dot(slope + slope.T, vectors, precision=FULL_PRECISION)


def body(
    hidden,
    skip_tokens,
    backbone_cotangent,
    head_cotangent,
    starts,
    positives,
    qkv_weight,
    qv_bias,
    attn_weight,
    attn_bias,
    attn_gain,
    attn_shift,
    inner_weight,
    inner_bias,
    outer_weight,
    outer_bias,
    ffn_gain,
    ffn_shift,
):
    rows_dev, local, width = hidden.shape
    grid = Grid(rows_dev)
    tokens = rows_dev * local
    length = tokens * grid.members

    starts_both = jnp.stack([starts, grid.swap(starts, grid.f_bits)])
    from_other = jnp.where(grid.row_in_group // rows_dev == grid.core, 0, 1)
    my_starts = lax.dynamic_index_in_dim(starts_both, from_other, 0, keepdims=False)
    my_starts = lax.dynamic_index_in_dim(
        my_starts, grid.row_in_group % rows_dev, 0, keepdims=False
    )
    place = jnp.arange(tokens, dtype=jnp.int32)
    q_pos = grid.member * tokens + place
    k_pos = jnp.concatenate(
        [
            (grid.member - shift) % grid.members * tokens + place
            for shift in range(grid.members)
        ]
    )
    segment = lambda pos: jnp.sum((my_starts[:, None] <= pos[None, :]).astype(jnp.int32), axis=0) - 1
    seg_q = segment(q_pos)[None, :]
    seg_k = segment(k_pos)[:, None]
    cls_hot = (my_starts[:, None] == q_pos[None, :]).astype(F32)
    is_cls = jnp.any(my_starts[:, None] == q_pos[None, :], axis=0)[:, None]

    devices = grid.n_dp * grid.n_f
    vectors = (qv_bias, attn_bias, attn_gain, attn_shift, inner_bias, outer_bias, ffn_gain, ffn_shift)
    sizes = [v.shape[1] for v in vectors]
    rows = qkv_weight.shape[1]
    small_own = jnp.concatenate(vectors, axis=1).reshape(rows, -1)
    small_cols = small_own.shape[1]
    padded = -(-small_cols // 128) * 128
    small_own = jnp.pad(small_own, ((0, 0), (0, padded - small_cols)))
    schedule = Schedule(PLAN)
    tick = schedule.tick

    def gather_qkv(*parts):
        out = jnp.concatenate(parts, axis=1)
        out = yield from grid.gather_z(out)
        return (yield from grid.gather_split(out))

    def gather_ffn(inner, outer):
        deep = outer.shape[0] // inner.shape[0]
        out = jnp.concatenate([inner, outer.reshape(inner.shape[0], -1)], axis=1)
        out = yield from grid.gather_z(out)
        inner, outer = out[:, : inner.shape[1]], out[:, inner.shape[1] :]
        return (yield from grid.gather_two(inner, outer.reshape(inner.shape[0] * deep, -1)))

    schedule.add(QKV_1, gather_qkv, lambda: (qkv_weight[0], attn_weight[0], small_own))
    schedule.add(QKV_2, gather_qkv, lambda: (qkv_weight[1], attn_weight[1]))
    schedule.add(FFN_1, gather_ffn, lambda: (inner_weight[0], outer_weight[0]))
    schedule.add(FFN_2, gather_ffn, lambda: (inner_weight[1], outer_weight[1]))
    schedule.add(HIDDEN, grid.to_rows, lambda: (hidden,))
    schedule.add(
        SKIP, grid.to_rows, lambda: (jnp.concatenate([skip_tokens, head_cotangent], axis=2),)
    )
    schedule.add(COTS, grid.to_rows, lambda: (backbone_cotangent,))

    small = []

    def weights_of(layer, qkv_name, ffn_name):
        def get(is_qkv):
            if not is_qkv:
                return schedule.get(ffn_name)
            if not small:
                every = schedule.get(QKV_1)[:, -padded:][:, :small_cols]
                small.append(every.reshape(devices, 2, -1))
            pack = schedule.get(qkv_name)
            cut = qkv_weight.shape[2]
            return (pack[:, :cut], pack[:, cut : cut + width], *split_small(small[0][:, layer], sizes))

        return get

    backbone, head = weights_of(0, QKV_1, FFN_1), weights_of(1, QKV_2, FFN_2)

    def scatter_qkv(*parts):
        out = jnp.concatenate(parts, axis=1)
        out = yield from grid.scatter_split(out)
        return (yield from grid.scatter_z(out))

    core_first = lambda turned: [grid.f_bits] + grid.upper(turned)

    def scatter_z(inner, outer):
        deep = outer.shape[0] // inner.shape[0]
        out = jnp.concatenate([inner, outer.reshape(inner.shape[0], -1)], axis=1)
        out = yield from grid.scatter_z(out)
        return out[:, : inner.shape[1]], out[:, inner.shape[1] :].reshape(out.shape[0] * deep, -1)

    kept_small = []

    def give_to(outer_name, inner_name, ffn_name, qkv_name, last):
        def pack(grad_qkv, grad_attn, vectors):
            if not last:
                return grad_qkv, grad_attn
            cut = [
                jnp.concatenate([v.reshape(devices, -1) for v in kept], axis=1)
                for kept in (vectors, kept_small[0])
            ]
            flat = jnp.stack(cut, axis=1).reshape(devices * rows, small_cols).astype(BF)
            return grad_qkv, grad_attn, jnp.pad(flat, ((0, 0), (0, padded - small_cols)))

        def give(which, *grads):
            if which == AT_D_OUTER:
                schedule.add(outer_name, lambda g: grid.scatter(g, core_first(False)), lambda: grads)
            elif which == AT_D_INNER:
                schedule.add(inner_name, lambda g: grid.scatter(g, core_first(True)), lambda: grads)
                both = lambda: [v.astype(BF) for v in schedule.finish(inner_name, outer_name)]
                schedule.add(ffn_name, scatter_z, both)
            else:
                kept_small.append(grads[2])
                schedule.add(qkv_name, scatter_qkv, lambda: pack(*grads))

        return give

    shared = n_bits(grid.chips_per_row)
    cls_bits = list(range(shared, grid.f_bits)) + grid.upper(True)

    def gather_cls(states):
        own = jnp.dot(cls_hot, states, precision=FULL_PRECISION)[None]
        for bit in [grid.f_bits] + list(range(shared)):
            got = yield grid.swap(own, bit)
            own = own + got
        return (yield from grid.gather(own, cls_bits))

    first_states = []
    schedule.add(CLS, gather_cls, lambda: (first_states[0],))

    mark = jnp.zeros((8, 128), F32) + my_starts[0].astype(F32)
    for n in range(START_TICKS):
        mark = tick((START, n), mark)
    x = schedule.get(HIDDEN)
    first, saved_one = layer_forward(grid, F0, tick, x, backbone, seg_q, seg_k, first_states)
    for n in range(BETWEEN_TICKS):
        first = tick((BETWEEN, n), first)
    skip_and_cot = schedule.get(SKIP)
    head_in = jnp.where(is_cls, first, skip_and_cot[:, :width].astype(F32))
    second, saved_two = layer_forward(grid, F1, tick, head_in, head, seg_q, seg_k)

    head_up = tick((TURN, 0), skip_and_cot[:, width:]).astype(F32)
    give = give_to(OUTER_G2, INNER_G2, FFN_G2, QKV_G2, False)
    d_head_in = layer_backward(grid, B1, tick, give, head_up, head, saved_two, seg_q, seg_k)
    skip_grad = jnp.where(is_cls, 0.0, d_head_in).astype(BF)
    results = jnp.concatenate([first.astype(BF), second.astype(BF), skip_grad], axis=1)
    schedule.add(OUTS, grid.from_rows, lambda: (results,))
    contrast_loss, d_cls_all = contrastive(schedule.get(CLS).reshape(-1, width), positives)
    my_row = grid.dp // CORES * (CORES * rows_dev) + grid.row_in_group
    d_cls = lax.dynamic_slice_in_dim(d_cls_all, my_row * SEGS, SEGS, 0)
    cot = schedule.get(COTS)
    upstream = (
        cot.astype(F32)
        + jnp.where(is_cls, d_head_in, 0.0)
        + lax.dot_general(cls_hot, d_cls, (((0,), (0,)), ((), ())), precision=FULL_PRECISION)
    )
    upstream = tick((UP, 0), upstream)
    give = give_to(OUTER_G1, INNER_G1, FFN_G1, QKV_G1, True)
    schedule.add(HIDDEN_BACK, grid.from_rows, lambda: (d_input[0].astype(BF),))
    d_input = []
    layer_backward(grid, B0, tick, give, upstream, backbone, saved_one, seg_q, seg_k, d_input)
    mark = jnp.zeros((8, 128), F32)
    for n in range(END_TICKS):
        mark = tick((END, n), mark)
    names = [HIDDEN_BACK, OUTS, FFN_G1, FFN_G2, QKV_G1, QKV_G2]
    hidden_back, outs, (inner_1, outer_1), (inner_2, outer_2), qkv_1, qkv_2 = schedule.finish(*names)

    cut = qkv_weight.shape[2]
    pair = lambda a, b: jnp.stack([a, b]).astype(F32)
    small_g = qkv_1[:, -padded:][:, :small_cols].reshape(2, -1).astype(F32)
    cuts, at = [], 0
    for size in sizes:
        cuts.append(small_g[:, at : at + size])
        at += size
    return (
        contrast_loss,
        outs[:, :, :width],
        outs[:, :, width : 2 * width],
        hidden_back.astype(F32),
        outs[:, :, 2 * width :].astype(F32),
        pair(qkv_1[:, :cut], qkv_2[:, :cut]),
        cuts[0],
        pair(qkv_1[:, cut : cut + width], qkv_2[:, cut : cut + width]),
        cuts[1],
        cuts[2],
        cuts[3],
        pair(inner_1, inner_2),
        cuts[4],
        pair(outer_1, outer_2),
        cuts[5],
        cuts[6],
        cuts[7],
    )


def solution(mesh):
    rows = P("dp", "fsdp", None)
    matrix = P(None, ("dp", "fsdp"), None)
    vector = P(None, ("dp", "fsdp"))
    params = (
        matrix,
        vector,
        matrix,
        vector,
        vector,
        vector,
        matrix,
        vector,
        matrix,
        vector,
        vector,
        vector,
    )
    return jax.shard_map(
        body,
        mesh=mesh,
        in_specs=(rows, rows, rows, rows, P("dp", None), P()) + params,
        out_specs=(P(), rows, rows, rows, rows) + params,
        check_vma=False,
    )
```
